128 devices in a mesh: dp: 16 (over z, x), tensor: 8 (over y, core).
Axes of the slice: x: 4, y: 4, z: 4, core: 2. Of those that a mesh axis runs over, the one named last changes fastest.
Arguments:
- grad_gate: bfloat16 [16, 2048, 7168], P('dp', 'tensor'), may hold values from -6 to 6
- grad_up: bfloat16 [16, 2048, 7168], P('dp', 'tensor'), may hold values from -6 to 6
- err_gate: bfloat16 [16, 2048, 7168], P('dp', 'tensor'), may hold values from -4 to 4
- err_up: bfloat16 [16, 2048, 7168], P('dp', 'tensor'), may hold values from -4 to 4
- q_gate: float32 [7168, 64], replicated, may hold values from -0.0625 to 0.0625
- q_up: float32 [7168, 64], replicated, may hold values from -0.0625 to 0.0625
Outputs:
- new_err_gate: bfloat16 [16, 2048, 7168], P('dp', 'tensor')
- new_err_up: bfloat16 [16, 2048, 7168], P('dp', 'tensor')
- new_q_gate: float32 [7168, 64], replicated
- new_q_up: float32 [7168, 64], replicated
The draws below stay inside these ranges and needn't reach their ends.
All inputs are finite; a program needn't handle non-finite values.
Results may differ from the reference program's by a relative error of at most 0.0013.
Values sent between devices are 32-bit elements; how exact they have to be, the bound alone decides.
A program may use at most 128 MiB of HBM per device.

```python
import jax
import jax.numpy as jnp
from jax import lax

D = 7168
ROWS = 2048
RANK = 64
N_DP = 16


def steps_of(stream_key, shape, split, least, high):
    def one(dim, shards_of):
        draws = jax.random.uniform(jax.random.fold_in(jax.random.fold_in(stream_key, 6), dim), (shards_of,), jnp.float32, least / len(split), high / len(split))
        return jnp.repeat(jnp.exp(draws), shape[dim] // shards_of).reshape((-1,) + (1,) * (len(shape) - dim - 1))

    loudness = one(*split[0])
    for cut in split[1:]:
        loudness = loudness * one(*cut)
    return loudness


def centred(own_key, extent, spread, limit, cuts=(), kind=jnp.bfloat16):
    entries = spread * jax.random.normal(own_key, extent, jnp.float32)
    if cuts:
        entries = entries * steps_of(own_key, extent, cuts, -0.22, 0.18)
    return jnp.clip(entries, -limit, limit).astype(kind)


def setup_inputs(seed: int = 0) -> dict:
    seeds = jax.random.split(jax.random.key(seed), 7)
    return {
        "grad_gate": centred(seeds[0], (N_DP, ROWS, D), 1.0, 6.0, ((0, 16), (1, 8))),
        "grad_up": centred(seeds[1], (N_DP, ROWS, D), 1.0, 6.0, ((0, 16), (1, 8))),
        "err_gate": centred(seeds[2], (N_DP, ROWS, D), 0.5, 4.0, ((0, 16), (1, 8))),
        "err_up": centred(seeds[3], (N_DP, ROWS, D), 0.5, 4.0, ((0, 16), (1, 8))),
        "q_gate": centred(seeds[4], (D, RANK), D ** -0.5, 0.0625, (), jnp.float32),
        "q_up": centred(seeds[5], (D, RANK), D ** -0.5, 0.0625, (), jnp.float32),
    }


def compress(grad, err, q_prev):
    hp = lax.Precision.HIGHEST
    mat = grad.astype(jnp.float32) + err.astype(jnp.float32)
    left = jnp.einsum('nrd,dk->rk', mat, q_prev, precision=hp)
    gram = jnp.dot(left.T, left, precision=hp)
    lower = jnp.linalg.cholesky(gram)
    ortho = lax.linalg.triangular_solve(lower, left, left_side=False, lower=True, transpose_a=True)
    new_q = jnp.einsum('nrd,rk->dk', mat, ortho, precision=hp) / N_DP
    approx = jnp.dot(ortho, new_q.T, precision=hp)
    return ((mat - approx[None]).astype(jnp.bfloat16), new_q)

def reference(grad_gate, grad_up, err_gate, err_up, q_gate, q_up):
    new_err_gate, new_q_gate = compress(grad_gate, err_gate, q_gate)
    new_err_up, new_q_up = compress(grad_up, err_up, q_up)
    return (new_err_gate, new_err_up, new_q_gate, new_q_up)
```

```python
import functools

import jax
import jax.numpy as jnp
from jax import lax
from jax.experimental import pallas as pl
from jax.experimental.pallas import tpu as pltpu
from jax.sharding import PartitionSpec as P

MESH = pl.DeviceIdType.MESH
F32 = jnp.float32
BF16 = jnp.bfloat16
HP = lax.Precision.HIGHEST

DP = 16
TENSOR = 8
D = 7168
ROWS = 256
RANK = 64
HALF = D // 2
CHUNKS = 4
CHUNK = D // CHUNKS
TILE = 256
PARTS = ((0, 1280), (1280, 1280), (2560, 1024))
STAGES = 7
CORE_SUM, A_SUM, B_SUM, C_SUM, B_ALL, A_ALL, CORE_ALL = range(STAGES)


def three(value):
    first = value.astype(BF16)
    rest = value - first.astype(F32)
    second = rest.astype(BF16)
    third = (rest - second.astype(F32)).astype(BF16)
    return first, second, third


def nt(left, right, precision=None):
    return lax.dot_general(
        left, right, (((1,), (1,)), ((), ())), precision=precision, preferred_element_type=F32
    )


def nn(left, right, precision=None):
    return jnp.dot(left, right, precision=precision, preferred_element_type=F32)


def exchange_kernel(
    grad_gate, err_gate, grad_up, err_up, q_gate, q_up,
    data, total, left, inverse,
    q_buf, p_acc, p_part, p_recv, p_stack, w_send, w_own, w_recv,
    a_recv0, a_recv1, a_recv2, a_sum0, a_sum1, a_sum2,
    b_recv0, b_recv1, b_recv2, c_recv0, c_recv1, c_recv2,
    g_part, g_recv, g_all, work, low,
    load_sem, p_send_sem, p_recv_sem, g_send_sem, g_recv_sem, w_send_sem, w_recv_sem,
):
    a_recv = (a_recv0, a_recv1, a_recv2)
    a_sum = (a_sum0, a_sum1, a_sum2)
    b_recv = (b_recv0, b_recv1, b_recv2)
    c_recv = (c_recv0, c_recv1, c_recv2)
    dp = lax.axis_index("dp")
    t = lax.axis_index("tensor")
    z, x = dp // 4, lax.rem(dp, 4)
    y, core = t // 2, lax.rem(t, 2)
    at = (x, y, z)

    def peer(axis, v):
        px, py, pz = (v if axis == i else at[i] for i in range(3))
        return (pz * 4 + px, py * 2 + core)

    def send(src, dst, send_sem, recv_sem, device):
        pltpu.make_async_remote_copy(
            src_ref=src, dst_ref=dst, send_sem=send_sem, recv_sem=recv_sem,
            device_id=device, device_id_type=MESH,
        ).start()

    def arrived(ref, sem):
        pltpu.make_async_copy(ref, ref, sem).wait()

    sources = ((q_gate, grad_gate, err_gate), (q_up, grad_up, err_up))

    def load(g, c, k):
        cols = pl.ds(c * CHUNK, CHUNK)
        if k == 0:
            dst = q_buf.at[g, :, cols]
        else:
            dst = data.at[pl.ds((2 * g + k - 1) * ROWS, ROWS), cols]
        return pltpu.make_async_copy(sources[g][k].at[:, cols], dst, load_sem.at[g, c, k])

    for g in range(2):
        for c in range(CHUNKS):
            for k in range(3):
                load(g, c, k).start()

    barrier = pltpu.get_barrier_semaphore()
    for d in range(1, DP):
        pl.semaphore_signal(
            barrier, inc=1, device_id=(lax.rem(dp + d, DP), t), device_id_type=MESH
        )
    for d in range(1, TENSOR):
        pl.semaphore_signal(
            barrier, inc=1, device_id=(dp, lax.rem(t + d, TENSOR)), device_id_type=MESH
        )

    def chunk_of(member):
        return pl.ds(pl.multiple_of(8 * (member // 2), 8), 8), pl.ds(
            pl.multiple_of(128 * lax.rem(member, 2), 128), 128
        )

    def p_compute(g):
        for c in range(CHUNKS):
            for k in range(3):
                load(g, c, k).wait()
            q3 = jnp.concatenate(three(q_buf[g, :, c * CHUNK : (c + 1) * CHUNK]), axis=0)
            both = nt(data[2 * g * ROWS : (2 * g + 2) * ROWS, c * CHUNK : (c + 1) * CHUNK], q3)
            if c == 0:
                p_acc[...] = both
            else:
                p_acc[...] += both
        both = p_acc[:ROWS, :] + p_acc[ROWS:, :]
        turned = both.T
        p_part[g] = turned[:RANK] + turned[RANK : 2 * RANK] + turned[2 * RANK :]

    def p_sum_start(g):
        for d in range(1, DP):
            member = lax.rem(dp + d, DP)
            rows, cols = chunk_of(member)
            send(
                p_part.at[g, rows, cols], p_recv.at[g, d - 1],
                p_send_sem.at[g, 0], p_recv_sem.at[g, 0], (member, t),
            )

    def p_all_start(g):
        arrived(p_recv.at[g], p_recv_sem.at[g, 0])
        rows, cols = chunk_of(dp)
        summed = p_part[g, rows, cols]
        for d in range(DP - 1):
            summed = summed + p_recv[g, d]
        left[g, rows, cols] = summed
        for d in range(1, DP):
            send(
                left.at[g, rows, cols], left.at[g, rows, cols],
                p_send_sem.at[g, 1], p_recv_sem.at[g, 1], (lax.rem(dp + d, DP), t),
            )

    def p_done(g):
        arrived(p_recv.at[g], p_recv_sem.at[g, 1])
        p3 = jnp.concatenate(three(left[g]), axis=0)
        p_stack[g, :, :ROWS] = p3
        p_stack[g, :, ROWS:] = p3

    def w_block(g, dst, half, p):
        first, width = PARTS[p]
        start = pl.multiple_of(half * HALF + first, 128)

        def step(i, carry):
            offset = pl.multiple_of(i * TILE, TILE)
            cols = pl.ds(pl.multiple_of(start + offset, 128), TILE)
            prod = nn(p_stack[g], data[pl.ds(2 * g * ROWS, 2 * ROWS), cols])
            dst[g, :, pl.ds(pl.multiple_of(first + offset, 128), TILE)] = (
                prod[:RANK] + prod[RANK : 2 * RANK] + prod[2 * RANK :]
            )
            return carry

        lax.fori_loop(0, width // TILE, step, 0)

    def sems(g, p, stage):
        return w_send_sem.at[g, p, stage], w_recv_sem.at[g, p, stage]

    def axes_of(g, p):
        first = (p + g) % 3
        return first, (first + 1) % 3, (first + 2) % 3

    def part_cols(p):
        return pl.ds(PARTS[p][0], PARTS[p][1])

    def total_block(g, p):
        a, _, _ = axes_of(g, p)
        first, width = PARTS[p]
        return total.at[
            g,
            pl.ds(pl.multiple_of(16 * at[a], 16), 16),
            pl.ds(pl.multiple_of(core * HALF + first, 128), width),
        ]

    def total_leaf(g, p):
        a, b, _ = axes_of(g, p)
        first, width = PARTS[p]
        row = 16 * at[a] + 8 * (at[b] // 2)
        col = core * HALF + first + (width // 2) * lax.rem(at[b], 2)
        return total.at[
            g, pl.ds(pl.multiple_of(row, 8), 8), pl.ds(pl.multiple_of(col, 128), width // 2)
        ]

    def core_start(g):
        for p in range(3):
            w_block(g, w_send, 1 - core, p)
            send(
                w_send.at[g, :, part_cols(p)], w_recv.at[g, :, part_cols(p)],
                *sems(g, p, CORE_SUM), (dp, y * 2 + 1 - core),
            )

    def a_start(g):
        for p in range(3):
            w_block(g, w_own, core, p)
            first, width = PARTS[p]
            cols = part_cols(p)
            arrived(w_recv.at[g, :, cols], w_recv_sem.at[g, p, CORE_SUM])
            w_own[g, :, cols] += w_recv[g, :, cols]
            a, _, _ = axes_of(g, p)
            for d in range(1, 4):
                v = lax.rem(at[a] + d, 4)
                send(
                    w_own.at[g, pl.ds(pl.multiple_of(16 * v, 16), 16), cols],
                    a_recv[p].at[g, d - 1],
                    *sems(g, p, A_SUM), peer(a, v),
                )

    def b_start(g):
        for p in range(3):
            a, b, _ = axes_of(g, p)
            first, width = PARTS[p]
            arrived(a_recv[p].at[g], w_recv_sem.at[g, p, A_SUM])
            a_sum[p][g] = (
                w_own[g, pl.ds(pl.multiple_of(16 * at[a], 16), 16), part_cols(p)]
                + a_recv[p][g, 0] + a_recv[p][g, 1] + a_recv[p][g, 2]
            )
            for d in range(1, 4):
                v = lax.rem(at[b] + d, 4)
                send(
                    a_sum[p].at[g, leaf_rows(v), leaf_cols(v, width)], b_recv[p].at[g, d - 1],
                    *sems(g, p, B_SUM), peer(b, v),
                )

    def leaf_rows(v):
        return pl.ds(pl.multiple_of(8 * (v // 2), 8), 8)

    def leaf_cols(v, width):
        return pl.ds(pl.multiple_of((width // 2) * lax.rem(v, 2), 128), width // 2)

    def c_start(g):
        for p in range(3):
            _, b, c = axes_of(g, p)
            first, width = PARTS[p]
            arrived(b_recv[p].at[g], w_recv_sem.at[g, p, B_SUM])
            c_recv[p][g, at[c]] = (
                a_sum[p][g, leaf_rows(at[b]), leaf_cols(at[b], width)]
                + b_recv[p][g, 0] + b_recv[p][g, 1] + b_recv[p][g, 2]
            )
            for d in range(1, 4):
                send(
                    c_recv[p].at[g, at[c]], c_recv[p].at[g, at[c]],
                    *sems(g, p, C_SUM), peer(c, lax.rem(at[c] + d, 4)),
                )

    def b_all_start(g):
        for p in range(3):
            _, b, _ = axes_of(g, p)
            arrived(c_recv[p].at[g, pl.ds(0, 3)], w_recv_sem.at[g, p, C_SUM])
            leaf = total_leaf(g, p)
            leaf[...] = c_recv[p][g, 0] + c_recv[p][g, 1] + c_recv[p][g, 2] + c_recv[p][g, 3]
            for d in range(1, 4):
                send(leaf, leaf, *sems(g, p, B_ALL), peer(b, lax.rem(at[b] + d, 4)))

    def a_all_start(g):
        for p in range(3):
            a, _, _ = axes_of(g, p)
            arrived(b_recv[p].at[g], w_recv_sem.at[g, p, B_ALL])
            block = total_block(g, p)
            for d in range(1, 4):
                send(block, block, *sems(g, p, A_ALL), peer(a, lax.rem(at[a] + d, 4)))

    def core_all_start(g):
        for p in range(3):
            first, width = PARTS[p]
            arrived(a_recv[p].at[g], w_recv_sem.at[g, p, A_ALL])
            part = total.at[g, :, pl.ds(pl.multiple_of(core * HALF + first, 128), width)]
            send(part, part, *sems(g, p, CORE_ALL), (dp, y * 2 + 1 - core))

    def core_all_done(g):
        for p in range(3):
            arrived(w_recv.at[g, :, part_cols(p)], w_recv_sem.at[g, p, CORE_ALL])

    member = lax.rem(dp, 8)
    mine = pl.ds(pl.multiple_of(8 * member, 8), 8)

    def gram_start():
        for g in range(2):
            g_part[:, g * RANK : (g + 1) * RANK] = nt(left[g], left[g], HP)
        for d in range(1, TENSOR):
            send(
                g_part.at[mine, :], g_recv.at[t],
                g_send_sem.at[0], g_recv_sem.at[0], (dp, lax.rem(t + d, TENSOR)),
            )
        g_recv[t] = g_part[mine, :]

    def gram_all_start():
        arrived(g_recv.at[pl.ds(0, 7)], g_recv_sem.at[0])
        summed = g_recv[0]
        for i in range(1, TENSOR):
            summed = summed + g_recv[i]
        g_all[mine, :] = summed
        for d in range(1, 8):
            other = 8 * (dp // 8) + lax.rem(member + d, 8)
            send(
                g_all.at[mine, :], g_all.at[mine, :],
                g_send_sem.at[1], g_recv_sem.at[1], (other, t),
            )

    lane = lax.broadcasted_iota(jnp.int32, (RANK, 2 * RANK), 1)
    row = lax.broadcasted_iota(jnp.int32, (RANK, 2 * RANK), 0)
    lane_one = lax.broadcasted_iota(jnp.int32, (1, 2 * RANK), 1)

    def gram_done():
        arrived(g_recv.at[pl.ds(0, 7)], g_recv_sem.at[1])
        work[...] = g_all[...]
        low[...] = jnp.where(lax.rem(lane, RANK) == row, 1.0, 0.0).astype(F32)

    def halves(value, lanes, column):
        gate = jnp.sum(jnp.where(lanes == column, value, 0.0), axis=1, keepdims=True)
        up = jnp.sum(jnp.where(lanes == column + RANK, value, 0.0), axis=1, keepdims=True)
        return jnp.where(lanes < RANK, gate, up)

    def eliminate(first, last):
        def step(j, carry):
            value = work[...]
            pivot_row = work[pl.ds(j, 1), :]
            low_row = low[pl.ds(j, 1), :]
            scale = 1.0 / halves(pivot_row, lane_one, j)
            factor = jnp.where(row > j, halves(value, lane, j) * scale, 0.0)
            work[...] = value - factor * pivot_row
            low[...] = low[...] - factor * low_row
            return carry

        lax.fori_loop(first, last, step, 0)

    def inverse_done():
        value = work[...]
        on = lax.rem(lane, RANK) == row
        gate = jnp.sum(jnp.where(on & (lane < RANK), value, 0.0), axis=1, keepdims=True)
        up = jnp.sum(jnp.where(on & (lane >= RANK), value, 0.0), axis=1, keepdims=True)
        diagonal = jnp.where(lane < RANK, gate, up)
        inverse[...] = low[...] / jnp.sqrt(diagonal)

    p_compute(0)
    pl.semaphore_wait(barrier, DP + TENSOR - 2)
    p_sum_start(0)
    p_compute(1)
    p_sum_start(1)
    p_all_start(0)
    p_all_start(1)
    p_done(0)
    core_start(0)
    a_start(0)
    p_done(1)
    gram_start()
    core_start(1)
    b_start(0)
    a_start(1)
    gram_all_start()
    c_start(0)
    b_start(1)
    gram_done()
    b_all_start(0)
    c_start(1)
    eliminate(0, 16)
    a_all_start(0)
    b_all_start(1)
    eliminate(16, 32)
    a_all_start(1)
    core_all_start(0)
    eliminate(32, RANK)
    inverse_done()
    core_all_start(1)
    core_all_done(0)
    core_all_done(1)

    for g in range(2):
        for phase in range(2):
            arrived(p_recv.at[g], p_send_sem.at[g, phase])
        for p in range(3):
            cols = part_cols(p)
            arrived(w_recv.at[g, :, cols], w_send_sem.at[g, p, CORE_SUM])
            arrived(w_recv.at[g, :, cols], w_send_sem.at[g, p, CORE_ALL])
            for stage in (A_SUM, A_ALL):
                arrived(a_recv[p].at[g], w_send_sem.at[g, p, stage])
            for stage in (B_SUM, C_SUM, B_ALL):
                arrived(b_recv[p].at[g], w_send_sem.at[g, p, stage])
    for phase in range(2):
        arrived(g_recv.at[pl.ds(0, 7)], g_send_sem.at[phase])


BLOCKS = 7
BLOCK = D // BLOCKS


def finish_kernel(
    data, total, left, inverse, new_err_gate, new_err_up, new_q_gate, new_q_up,
    err_stage, q_stage, low_stack, ortho_stack, sem,
):
    err_out = (new_err_gate, new_err_up)
    q_out = (new_q_gate, new_q_up)
    for g in range(2):
        low = inverse[:, g * RANK : (g + 1) * RANK]
        column = jnp.concatenate(three(low), axis=0)
        low_stack[g] = jnp.concatenate([column, column, column], axis=1)
        ortho = nn(low, left[g], HP).T
        first = ortho.astype(BF16).astype(F32)
        second = ortho - first
        ortho_stack[g] = jnp.concatenate([first, first, second, second], axis=1).astype(BF16)

    def copies(g, cols):
        return (
            pltpu.make_async_copy(err_stage.at[g, :, cols], err_out[g].at[:, cols], sem.at[g, 0]),
            pltpu.make_async_copy(q_stage.at[g, :, cols], q_out[g].at[:, cols], sem.at[g, 1]),
        )

    def step(i, carry):
        cols = pl.ds(pl.multiple_of(i * BLOCK, BLOCK), BLOCK)
        for g in range(2):
            summed = jnp.concatenate(three(total[g, :, cols]), axis=0)
            terms = nn(low_stack[g], summed)
            new_q = (terms[:RANK] + terms[RANK : 2 * RANK] + terms[2 * RANK :]) * (1.0 / DP)
            q_stage[g, :, cols] = new_q
            first = new_q.astype(BF16)
            second = (new_q - first.astype(F32)).astype(BF16)
            approx = nn(
                ortho_stack[g], jnp.concatenate([first, second, first, second], axis=0)
            )
            grad = data[pl.ds(2 * g * ROWS, ROWS), cols].astype(F32)
            err = data[pl.ds((2 * g + 1) * ROWS, ROWS), cols].astype(F32)
            err_stage[g, :, cols] = (grad + err - approx).astype(BF16)
            for copy in copies(g, cols):
                copy.start()
        return carry

    lax.fori_loop(0, BLOCKS, step, 0)
    for g in range(2):
        for copy in copies(g, pl.ds(0, D)):
            copy.wait()


def body(grad_gate, grad_up, err_gate, err_up, q_gate, q_up):
    def part_scratch(*lead):
        def of(divide, rows):
            return [pltpu.VMEM(lead + (rows, width // divide), F32) for _, width in PARTS]

        return of

    data, total, left, inverse = pl.pallas_call(
        exchange_kernel,
        out_shape=(
            pltpu.VMEM((4 * ROWS, D), BF16),
            pltpu.VMEM((2, RANK, D), F32),
            pltpu.VMEM((2, RANK, ROWS), F32),
            pltpu.VMEM((RANK, 2 * RANK), F32),
        ),
        in_specs=[pl.BlockSpec(memory_space=pl.ANY)] * 6,
        out_specs=[pl.BlockSpec(memory_space=pltpu.VMEM)] * 4,
        scratch_shapes=[
            pltpu.VMEM((2, RANK, D), F32),
            pltpu.VMEM((2 * ROWS, 3 * RANK), F32),
            pltpu.VMEM((2, RANK, ROWS), F32),
            pltpu.VMEM((2, DP - 1, 8, 128), F32),
            pltpu.VMEM((2, 3 * RANK, 2 * ROWS), BF16),
            pltpu.VMEM((2, RANK, HALF), F32),
            pltpu.VMEM((2, RANK, HALF), F32),
            pltpu.VMEM((2, RANK, HALF), F32),
            *part_scratch(2, 3)(1, 16),
            *part_scratch(2)(1, 16),
            *part_scratch(2, 3)(2, 8),
            *part_scratch(2, 4)(2, 8),
            pltpu.VMEM((RANK, 2 * RANK), F32),
            pltpu.VMEM((TENSOR, 8, 2 * RANK), F32),
            pltpu.VMEM((RANK, 2 * RANK), F32),
            pltpu.VMEM((RANK, 2 * RANK), F32),
            pltpu.VMEM((RANK, 2 * RANK), F32),
            pltpu.SemaphoreType.DMA((2, CHUNKS, 3)),
            pltpu.SemaphoreType.DMA((2, 2)),
            pltpu.SemaphoreType.DMA((2, 2)),
            pltpu.SemaphoreType.DMA((2,)),
            pltpu.SemaphoreType.DMA((2,)),
            pltpu.SemaphoreType.DMA((2, 3, STAGES)),
            pltpu.SemaphoreType.DMA((2, 3, STAGES)),
        ],
        compiler_params=pltpu.CompilerParams(
            collective_id=0, has_side_effects=True, vmem_limit_bytes=20 * 2**20
        ),
        name="exchange",
    )(
        *(
            pltpu.with_memory_space_constraint(v, pltpu.HBM)
            for v in (
                grad_gate.reshape(ROWS, D), err_gate.reshape(ROWS, D),
                grad_up.reshape(ROWS, D), err_up.reshape(ROWS, D), q_gate.T, q_up.T,
            )
        )
    )
    held = [pltpu.with_memory_space_constraint(v, pltpu.VMEM) for v in (data, total, left, inverse)]
    new_err_gate, new_err_up, new_q_gate, new_q_up = pl.pallas_call(
        finish_kernel,
        out_shape=(
            jax.ShapeDtypeStruct((ROWS, D), BF16),
            jax.ShapeDtypeStruct((ROWS, D), BF16),
            jax.ShapeDtypeStruct((RANK, D), F32),
            jax.ShapeDtypeStruct((RANK, D), F32),
        ),
        in_specs=[pl.BlockSpec(memory_space=pltpu.VMEM)] * 4,
        out_specs=[pl.BlockSpec(memory_space=pl.ANY)] * 4,
        scratch_shapes=[
            pltpu.VMEM((2, ROWS, D), BF16),
            pltpu.VMEM((2, RANK, D), F32),
            pltpu.VMEM((2, 3 * RANK, 3 * RANK), BF16),
            pltpu.VMEM((2, ROWS, 4 * RANK), BF16),
            pltpu.SemaphoreType.DMA((2, 2)),
        ],
        compiler_params=pltpu.CompilerParams(vmem_limit_bytes=16 * 2**20),
        name="finish",
    )(*held)
    return (
        new_err_gate.reshape(1, ROWS, D),
        new_err_up.reshape(1, ROWS, D),
        new_q_gate.T,
        new_q_up.T,
    )


def solution(mesh):
    placed = P("dp", "tensor", None)
    return jax.shard_map(
        body,
        mesh=mesh,
        in_specs=(placed, placed, placed, placed, P(), P()),
        out_specs=(placed, placed, P(), P()),
        check_vma=False,
    )
```

```python
import functools

import jax
import jax.numpy as jnp
from jax import lax
from jax.experimental import pallas as pl
from jax.experimental.pallas import tpu as pltpu
from jax.sharding import PartitionSpec as P

MESH = pl.DeviceIdType.MESH
F32 = jnp.float32
BF16 = jnp.bfloat16
HP = lax.Precision.HIGHEST

DP = 16
TENSOR = 8
D = 7168
ROWS = 256
RANK = 64
HALF = D // 2
CHUNKS = 4
CHUNK = D // CHUNKS
TILE = 256
PARTS = ((0, 1280), (1280, 1280), (2560, 1024))
BLOCKS = 4
BLOCK = D // BLOCKS
STAGES = 7
CORE_SUM, A_SUM, B_SUM, C_SUM, B_ALL, A_ALL, CORE_ALL = range(STAGES)


def three(value):
    first = value.astype(BF16)
    rest = value - first.astype(F32)
    second = rest.astype(BF16)
    third = (rest - second.astype(F32)).astype(BF16)
    return first, second, third


def nt(left, right, precision=None):
    return lax.dot_general(
        left, right, (((1,), (1,)), ((), ())), precision=precision, preferred_element_type=F32
    )


def nn(left, right, precision=None):
    return jnp.dot(left, right, precision=precision, preferred_element_type=F32)


def finish_stacks(low, left, low_stack, ortho_stack):
    column = jnp.concatenate(three(low), axis=0)
    low_stack[...] = jnp.concatenate([column, column, column], axis=1)
    ortho = nn(low, left, HP).T
    first = ortho.astype(BF16).astype(F32)
    second = ortho - first
    ortho_stack[...] = jnp.concatenate([first, first, second, second], axis=1).astype(BF16)


def finish_block(cols, data, total, low_stack, ortho_stack, err_out, q_out):
    summed = jnp.concatenate(three(total[:, cols]), axis=0)
    terms = nn(low_stack[...], summed)
    new_q = (terms[:RANK] + terms[RANK : 2 * RANK] + terms[2 * RANK :]) * (1.0 / DP)
    q_out[:, cols] = new_q
    first = new_q.astype(BF16)
    second = (new_q - first.astype(F32)).astype(BF16)
    approx = nn(ortho_stack[...], jnp.concatenate([first, second, first, second], axis=0))
    grad = data[:ROWS, cols].astype(F32)
    err = data[ROWS:, cols].astype(F32)
    err_out[:, cols] = (grad + err - approx).astype(BF16)


def exchange_kernel(
    grad_gate, err_gate, grad_up, err_up, q_gate, q_up,
    err_gate_out, q_gate_out, data_up, total_up, left, inverse,
    data_gate, total_gate, low_stack, ortho_stack,
    q_buf, p_acc, p_recv, p_stack, w_send, w_own, w_recv,
    a_recv0, a_recv1, a_recv2, a_sum0, a_sum1, a_sum2,
    b_recv0, b_recv1, b_recv2, c_recv0, c_recv1, c_recv2,
    g_part, g_recv, g_all, work, low,
    load_sem, p_send_sem, p_recv_sem, g_send_sem, g_recv_sem, w_send_sem, w_recv_sem,
):
    data = (data_gate, data_up)
    total = (total_gate, total_up)
    a_recv = (a_recv0, a_recv1, a_recv2)
    a_sum = (a_sum0, a_sum1, a_sum2)
    b_recv = (b_recv0, b_recv1, b_recv2)
    c_recv = (c_recv0, c_recv1, c_recv2)
    dp = lax.axis_index("dp")
    t = lax.axis_index("tensor")
    z, x = dp // 4, lax.rem(dp, 4)
    y, core = t // 2, lax.rem(t, 2)
    at = (x, y, z)
    one = dp // DP + 1

    def block(fn, *args):
        lax.fori_loop(0, one, lambda i, carry: (fn(*args), carry)[1], 0)

    def peer(axis, v):
        px, py, pz = (v if axis == i else at[i] for i in range(3))
        return (pz * 4 + px, py * 2 + core)

    def send(src, dst, send_sem, recv_sem, device):
        pltpu.make_async_remote_copy(
            src_ref=src, dst_ref=dst, send_sem=send_sem, recv_sem=recv_sem,
            device_id=device, device_id_type=MESH,
        ).start()

    def arrived(ref, sem):
        pltpu.make_async_copy(ref, ref, sem).wait()

    sources = ((q_gate, grad_gate, err_gate), (q_up, grad_up, err_up))

    def load(g, c, k):
        cols = pl.ds(pl.multiple_of(c * CHUNK, CHUNK), CHUNK)
        if k == 0:
            dst = q_buf.at[g, :, cols]
        else:
            dst = data[g].at[pl.ds((k - 1) * ROWS, ROWS), cols]
        return pltpu.make_async_copy(sources[g][k].at[:, cols], dst, load_sem.at[g, c, k])

    for g in range(2):
        for c in range(CHUNKS):
            for k in range(3):
                load(g, c, k).start()

    barrier = pltpu.get_barrier_semaphore()
    for d in range(1, DP):
        pl.semaphore_signal(
            barrier, inc=1, device_id=(lax.rem(dp + d, DP), t), device_id_type=MESH
        )
    for d in range(1, TENSOR):
        pl.semaphore_signal(
            barrier, inc=1, device_id=(dp, lax.rem(t + d, TENSOR)), device_id_type=MESH
        )

    def p_compute(g):
        p_acc[...] = jnp.zeros_like(p_acc)

        def step(c, carry):
            for k in range(3):
                load(g, c, k).wait()
            cols = pl.ds(pl.multiple_of(c * CHUNK, CHUNK), CHUNK)
            q3 = jnp.concatenate(three(q_buf[g, :, cols]), axis=0)
            p_acc[...] += nt(data[g][:, cols], q3)
            return carry

        lax.fori_loop(0, CHUNKS, step, 0)
        both = p_acc[:ROWS, :] + p_acc[ROWS:, :]
        turned = both.T
        summed = turned[:RANK] + turned[RANK : 2 * RANK] + turned[2 * RANK :]
        p_recv[g, 0, 0, x] = summed[: RANK // 2]
        p_recv[g, 0, 1, z] = summed[RANK // 2 :]

    def p_axis(step, h):
        return 0 if step == h else 2

    def p_start(g, step):
        for h in range(2):
            axis = p_axis(step, h)
            mine = p_recv.at[g, step, h, at[axis]]
            for d in range(1, 4):
                send(
                    mine, mine, p_send_sem.at[g, step, h], p_recv_sem.at[g, step, h],
                    peer(axis, lax.rem(at[axis] + d, 4)),
                )

    def p_sum(g, step, h):
        arrived(p_recv.at[g, step, h, pl.ds(0, 3)], p_recv_sem.at[g, step, h])
        return (
            p_recv[g, step, h, 0] + p_recv[g, step, h, 1]
            + p_recv[g, step, h, 2] + p_recv[g, step, h, 3]
        )

    def p_turn(g):
        for h in range(2):
            p_recv[g, 1, h, at[p_axis(1, h)]] = p_sum(g, 0, h)
        p_start(g, 1)

    def p_done(g):
        for h in range(2):
            left[g, h * (RANK // 2) : (h + 1) * (RANK // 2)] = p_sum(g, 1, h)
        p3 = jnp.concatenate(three(left[g]), axis=0)
        p_stack[g, :, :ROWS] = p3
        p_stack[g, :, ROWS:] = p3

    def w_block(g, dst, half, p):
        first, width = PARTS[p]
        start = pl.multiple_of(half * HALF + first, 128)

        for i in range(width // TILE):
            cols = pl.ds(pl.multiple_of(start + i * TILE, 128), TILE)
            prod = nn(p_stack[g], data[g][:, cols])
            dst[g, :, first + i * TILE : first + (i + 1) * TILE] = (
                prod[:RANK] + prod[RANK : 2 * RANK] + prod[2 * RANK :]
            )

    def sems(g, p, stage):
        return w_send_sem.at[g, p, stage], w_recv_sem.at[g, p, stage]

    def axes_of(g, p):
        first = (p + g) % 3
        return first, (first + 1) % 3, (first + 2) % 3

    def part_cols(p):
        return pl.ds(PARTS[p][0], PARTS[p][1])

    def total_block(g, p):
        a, _, _ = axes_of(g, p)
        first, width = PARTS[p]
        return total[g].at[
            pl.ds(pl.multiple_of(16 * at[a], 16), 16),
            pl.ds(pl.multiple_of(core * HALF + first, 128), width),
        ]

    def total_leaf(g, p):
        a, b, _ = axes_of(g, p)
        first, width = PARTS[p]
        row = 16 * at[a] + 8 * (at[b] // 2)
        col = core * HALF + first + (width // 2) * lax.rem(at[b], 2)
        return total[g].at[
            pl.ds(pl.multiple_of(row, 8), 8), pl.ds(pl.multiple_of(col, 128), width // 2)
        ]

    def core_start(g):
        for p in range(3):
            w_block(g, w_send, 1 - core, p)
            send(
                w_send.at[g, :, part_cols(p)], w_recv.at[g, :, part_cols(p)],
                *sems(g, p, CORE_SUM), (dp, y * 2 + 1 - core),
            )

    def w_rest(g):
        for p in range(3):
            w_block(g, w_own, core, p)

    def a_start(g):
        def step(p):
            cols = part_cols(p)
            arrived(w_recv.at[g, :, cols], w_recv_sem.at[g, p, CORE_SUM])
            w_own[g, :, cols] += w_recv[g, :, cols]
            a, _, _ = axes_of(g, p)
            for d in range(1, 4):
                v = lax.rem(at[a] + d, 4)
                send(
                    w_own.at[g, pl.ds(pl.multiple_of(16 * v, 16), 16), cols],
                    a_recv[p].at[g, d - 1],
                    *sems(g, p, A_SUM), peer(a, v),
                )

        for p in range(3):
            block(step, p)

    def b_start(g):
        def step(p):
            a, b, _ = axes_of(g, p)
            first, width = PARTS[p]
            arrived(a_recv[p].at[g], w_recv_sem.at[g, p, A_SUM])
            a_sum[p][g] = (
                w_own[g, pl.ds(pl.multiple_of(16 * at[a], 16), 16), part_cols(p)]
                + a_recv[p][g, 0] + a_recv[p][g, 1] + a_recv[p][g, 2]
            )
            for d in range(1, 4):
                v = lax.rem(at[b] + d, 4)
                send(
                    a_sum[p].at[g, leaf_rows(v), leaf_cols(v, width)], b_recv[p].at[g, d - 1],
                    *sems(g, p, B_SUM), peer(b, v),
                )

        for p in range(3):
            block(step, p)

    def leaf_rows(v):
        return pl.ds(pl.multiple_of(8 * (v // 2), 8), 8)

    def leaf_cols(v, width):
        return pl.ds(pl.multiple_of((width // 2) * lax.rem(v, 2), 128), width // 2)

    def c_start(g):
        def step(p):
            _, b, c = axes_of(g, p)
            first, width = PARTS[p]
            arrived(b_recv[p].at[g], w_recv_sem.at[g, p, B_SUM])
            c_recv[p][g, at[c]] = (
                a_sum[p][g, leaf_rows(at[b]), leaf_cols(at[b], width)]
                + b_recv[p][g, 0] + b_recv[p][g, 1] + b_recv[p][g, 2]
            )
            for d in range(1, 4):
                send(
                    c_recv[p].at[g, at[c]], c_recv[p].at[g, at[c]],
                    *sems(g, p, C_SUM), peer(c, lax.rem(at[c] + d, 4)),
                )

        for p in range(3):
            block(step, p)

    def b_all_start(g):
        def step(p):
            _, b, _ = axes_of(g, p)
            arrived(c_recv[p].at[g, pl.ds(0, 3)], w_recv_sem.at[g, p, C_SUM])
            leaf = total_leaf(g, p)
            leaf[...] = c_recv[p][g, 0] + c_recv[p][g, 1] + c_recv[p][g, 2] + c_recv[p][g, 3]
            for d in range(1, 4):
                send(leaf, leaf, *sems(g, p, B_ALL), peer(b, lax.rem(at[b] + d, 4)))

        for p in range(3):
            block(step, p)

    def a_all_start(g):
        def step(p):
            a, _, _ = axes_of(g, p)
            arrived(b_recv[p].at[g], w_recv_sem.at[g, p, B_ALL])
            block = total_block(g, p)
            for d in range(1, 4):
                send(block, block, *sems(g, p, A_ALL), peer(a, lax.rem(at[a] + d, 4)))

        for p in range(3):
            block(step, p)

    def core_all_start(g):
        def step(p):
            first, width = PARTS[p]
            arrived(a_recv[p].at[g], w_recv_sem.at[g, p, A_ALL])
            part = total[g].at[:, pl.ds(pl.multiple_of(core * HALF + first, 128), width)]
            send(part, part, *sems(g, p, CORE_ALL), (dp, y * 2 + 1 - core))

        for p in range(3):
            block(step, p)

    def core_all_done(g):
        for p in range(3):
            arrived(w_recv.at[g, :, part_cols(p)], w_recv_sem.at[g, p, CORE_ALL])

    member = lax.rem(dp, 8)
    mine = pl.ds(pl.multiple_of(8 * member, 8), 8)

    def gram_start():
        for g in range(2):
            g_part[:, g * RANK : (g + 1) * RANK] = nt(left[g], left[g], HP)
        for d in range(1, TENSOR):
            send(
                g_part.at[mine, :], g_recv.at[t],
                g_send_sem.at[0], g_recv_sem.at[0], (dp, lax.rem(t + d, TENSOR)),
            )
        g_recv[t] = g_part[mine, :]

    def gram_all_start():
        arrived(g_recv.at[pl.ds(0, 7)], g_recv_sem.at[0])
        summed = g_recv[0]
        for i in range(1, TENSOR):
            summed = summed + g_recv[i]
        g_all[mine, :] = summed
        for d in range(1, 8):
            other = 8 * (dp // 8) + lax.rem(member + d, 8)
            send(
                g_all.at[mine, :], g_all.at[mine, :],
                g_send_sem.at[1], g_recv_sem.at[1], (other, t),
            )

    lane = lax.broadcasted_iota(jnp.int32, (RANK, 2 * RANK), 1)
    row = lax.broadcasted_iota(jnp.int32, (RANK, 2 * RANK), 0)
    lane_one = lax.broadcasted_iota(jnp.int32, (1, 2 * RANK), 1)

    def gram_done():
        arrived(g_recv.at[pl.ds(0, 7)], g_recv_sem.at[1])
        work[...] = g_all[...]
        low[...] = jnp.where(lax.rem(lane, RANK) == row, 1.0, 0.0).astype(F32)

    def halves(value, lanes, column):
        gate = jnp.sum(jnp.where(lanes == column, value, 0.0), axis=1, keepdims=True)
        up = jnp.sum(jnp.where(lanes == column + RANK, value, 0.0), axis=1, keepdims=True)
        return jnp.where(lanes < RANK, gate, up)

    def eliminate(first, last):
        def step(j, carry):
            value = work[...]
            pivot_row = work[pl.ds(j, 1), :]
            low_row = low[pl.ds(j, 1), :]
            scale = 1.0 / halves(pivot_row, lane_one, j)
            factor = jnp.where(row > j, halves(value, lane, j) * scale, 0.0)
            work[...] = value - factor * pivot_row
            low[...] = low[...] - factor * low_row
            return carry

        lax.fori_loop(first, last, step, 0)

    def inverse_done():
        value = work[...]
        on = lax.rem(lane, RANK) == row
        gate = jnp.sum(jnp.where(on & (lane < RANK), value, 0.0), axis=1, keepdims=True)
        up = jnp.sum(jnp.where(on & (lane >= RANK), value, 0.0), axis=1, keepdims=True)
        diagonal = jnp.where(lane < RANK, gate, up)
        inverse[...] = low[...] / jnp.sqrt(diagonal)

    def finish_gate():
        finish_stacks(inverse[:, :RANK], left[0], low_stack, ortho_stack)
        for i in range(BLOCKS):
            finish_block(
                slice(i * BLOCK, (i + 1) * BLOCK), data_gate, total_gate, low_stack, ortho_stack,
                err_gate_out, q_gate_out,
            )

    p_compute(0)
    pl.semaphore_wait(barrier, DP + TENSOR - 2)
    p_start(0, 0)
    p_compute(1)
    p_start(1, 0)
    block(p_turn, 0)
    block(p_turn, 1)
    block(p_done, 0)
    block(core_start, 0)
    block(w_rest, 0)
    a_start(0)
    block(p_done, 1)
    block(core_start, 1)
    block(gram_start)
    block(w_rest, 1)
    b_start(0)
    a_start(1)
    block(gram_all_start)
    c_start(0)
    b_start(1)
    block(gram_done)
    b_all_start(0)
    eliminate(0, 8)
    c_start(1)
    eliminate(8, 24)
    a_all_start(0)
    b_all_start(1)
    eliminate(24, 40)
    a_all_start(1)
    eliminate(40, RANK)
    block(inverse_done)
    core_all_start(0)
    core_all_done(0)
    block(finish_gate)
    core_all_start(1)
    core_all_done(1)

    for g in range(2):
        for step in range(2):
            for h in range(2):
                arrived(p_recv.at[g, step, h, pl.ds(0, 3)], p_send_sem.at[g, step, h])
        for p in range(3):
            cols = part_cols(p)
            arrived(w_recv.at[g, :, cols], w_send_sem.at[g, p, CORE_SUM])
            arrived(w_recv.at[g, :, cols], w_send_sem.at[g, p, CORE_ALL])
            for stage in (A_SUM, A_ALL):
                arrived(a_recv[p].at[g], w_send_sem.at[g, p, stage])
            for stage in (B_SUM, C_SUM, B_ALL):
                arrived(b_recv[p].at[g], w_send_sem.at[g, p, stage])
    for phase in range(2):
        arrived(g_recv.at[pl.ds(0, 7)], g_send_sem.at[phase])


def finish_kernel(
    err_gate, q_gate, data, total, left, inverse,
    new_err_gate, new_err_up, new_q_gate, new_q_up,
    err_up, q_up, low_stack, ortho_stack, sem,
):
    gate = (
        pltpu.make_async_copy(err_gate, new_err_gate, sem.at[0]),
        pltpu.make_async_copy(q_gate, new_q_gate, sem.at[1]),
    )
    for copy in gate:
        copy.start()
    finish_stacks(inverse[:, RANK:], left[1], low_stack, ortho_stack)

    def copies(i):
        cols = pl.ds(pl.multiple_of(i * BLOCK, BLOCK), BLOCK)
        return (
            pltpu.make_async_copy(err_up.at[:, cols], new_err_up.at[:, cols], sem.at[2]),
            pltpu.make_async_copy(q_up.at[:, cols], new_q_up.at[:, cols], sem.at[3]),
        )

    def step(i, carry):
        finish_block(
            pl.ds(pl.multiple_of(i * BLOCK, BLOCK), BLOCK), data, total, low_stack, ortho_stack,
            err_up, q_up,
        )
        for copy in copies(i):
            copy.start()
        return carry

    lax.fori_loop(0, BLOCKS, step, 0)
    for copy in gate:
        copy.wait()
    pltpu.make_async_copy(err_up, new_err_up, sem.at[2]).wait()
    pltpu.make_async_copy(q_up, new_q_up, sem.at[3]).wait()


def body(grad_gate, grad_up, err_gate, err_up, q_gate, q_up):
    def part_scratch(*lead):
        def of(divide, rows):
            return [pltpu.VMEM(lead + (rows, width // divide), F32) for _, width in PARTS]

        return of

    made = pl.pallas_call(
        exchange_kernel,
        out_shape=(
            pltpu.VMEM((ROWS, D), BF16),
            pltpu.VMEM((RANK, D), F32),
            pltpu.VMEM((2 * ROWS, D), BF16),
            pltpu.VMEM((RANK, D), F32),
            pltpu.VMEM((2, RANK, ROWS), F32),
            pltpu.VMEM((RANK, 2 * RANK), F32),
        ),
        in_specs=[pl.BlockSpec(memory_space=pl.ANY)] * 6,
        out_specs=[pl.BlockSpec(memory_space=pltpu.VMEM)] * 6,
        scratch_shapes=[
            pltpu.VMEM((2 * ROWS, D), BF16),
            pltpu.VMEM((RANK, D), F32),
            pltpu.VMEM((3 * RANK, 3 * RANK), BF16),
            pltpu.VMEM((ROWS, 4 * RANK), BF16),
            pltpu.VMEM((2, RANK, D), F32),
            pltpu.VMEM((2 * ROWS, 3 * RANK), F32),
            pltpu.VMEM((2, 2, 2, 4, RANK // 2, ROWS), F32),
            pltpu.VMEM((2, 3 * RANK, 2 * ROWS), BF16),
            pltpu.VMEM((2, RANK, HALF), F32),
            pltpu.VMEM((2, RANK, HALF), F32),
            pltpu.VMEM((2, RANK, HALF), F32),
            *part_scratch(2, 3)(1, 16),
            *part_scratch(2)(1, 16),
            *part_scratch(2, 3)(2, 8),
            *part_scratch(2, 4)(2, 8),
            pltpu.VMEM((RANK, 2 * RANK), F32),
            pltpu.VMEM((TENSOR, 8, 2 * RANK), F32),
            pltpu.VMEM((RANK, 2 * RANK), F32),
            pltpu.VMEM((RANK, 2 * RANK), F32),
            pltpu.VMEM((RANK, 2 * RANK), F32),
            pltpu.SemaphoreType.DMA((2, CHUNKS, 3)),
            pltpu.SemaphoreType.DMA((2, 2, 2)),
            pltpu.SemaphoreType.DMA((2, 2, 2)),
            pltpu.SemaphoreType.DMA((2,)),
            pltpu.SemaphoreType.DMA((2,)),
            pltpu.SemaphoreType.DMA((2, 3, STAGES)),
            pltpu.SemaphoreType.DMA((2, 3, STAGES)),
        ],
        compiler_params=pltpu.CompilerParams(
            collective_id=0, has_side_effects=True, vmem_limit_bytes=32 * 2**20
        ),
        name="exchange",
    )(
        *(
            pltpu.with_memory_space_constraint(v, pltpu.HBM)
            for v in (
                grad_gate.reshape(ROWS, D), err_gate.reshape(ROWS, D),
                grad_up.reshape(ROWS, D), err_up.reshape(ROWS, D), q_gate.T, q_up.T,
            )
        )
    )
    held = [pltpu.with_memory_space_constraint(v, pltpu.VMEM) for v in made]
    new_err_gate, new_err_up, new_q_gate, new_q_up = pl.pallas_call(
        finish_kernel,
        out_shape=(
            jax.ShapeDtypeStruct((ROWS, D), BF16),
            jax.ShapeDtypeStruct((ROWS, D), BF16),
            jax.ShapeDtypeStruct((RANK, D), F32),
            jax.ShapeDtypeStruct((RANK, D), F32),
        ),
        in_specs=[pl.BlockSpec(memory_space=pltpu.VMEM)] * 6,
        out_specs=[pl.BlockSpec(memory_space=pl.ANY)] * 4,
        scratch_shapes=[
            pltpu.VMEM((ROWS, D), BF16),
            pltpu.VMEM((RANK, D), F32),
            pltpu.VMEM((3 * RANK, 3 * RANK), BF16),
            pltpu.VMEM((ROWS, 4 * RANK), BF16),
            pltpu.SemaphoreType.DMA((4,)),
        ],
        compiler_params=pltpu.CompilerParams(vmem_limit_bytes=12 * 2**20),
        name="finish",
    )(*held)
    return (
        new_err_gate.reshape(1, ROWS, D),
        new_err_up.reshape(1, ROWS, D),
        new_q_gate.T,
        new_q_up.T,
    )


def solution(mesh):
    placed = P("dp", "tensor", None)
    return jax.shard_map(
        body,
        mesh=mesh,
        in_specs=(placed, placed, placed, placed, P(), P()),
        out_specs=(placed, placed, P(), P()),
        check_vma=False,
    )
```

```python
import functools

import jax
import jax.numpy as jnp
from jax import lax
from jax.experimental import pallas as pl
from jax.experimental.pallas import tpu as pltpu
from jax.sharding import PartitionSpec as P

MESH = pl.DeviceIdType.MESH
F32 = jnp.float32
BF16 = jnp.bfloat16
HP = lax.Precision.HIGHEST

DP = 16
TENSOR = 8
D = 7168
ROWS = 256
RANK = 64
HALF = D // 2
CHUNKS = 4
CHUNK = D // CHUNKS
TILE = 256
PARTS = ((0, 1280), (1280, 1280), (2560, 1024))
BLOCKS = 4
BLOCK = D // BLOCKS
STAGES = 7
CORE_SUM, A_SUM, B_SUM, C_SUM, B_ALL, A_ALL, CORE_ALL = range(STAGES)


def three(value):
    first = value.astype(BF16)
    rest = value - first.astype(F32)
    second = rest.astype(BF16)
    third = (rest - second.astype(F32)).astype(BF16)
    return first, second, third


def nt(left, right, precision=None):
    return lax.dot_general(
        left, right, (((1,), (1,)), ((), ())), precision=precision, preferred_element_type=F32
    )


def nn(left, right, precision=None):
    return jnp.dot(left, right, precision=precision, preferred_element_type=F32)


def finish_stacks(low, left, low_stack, ortho_stack):
    column = jnp.concatenate(three(low), axis=0)
    low_stack[...] = jnp.concatenate([column, column, column], axis=1)
    ortho = nn(low, left, HP).T
    first = ortho.astype(BF16).astype(F32)
    second = ortho - first
    ortho_stack[...] = jnp.concatenate([first, first, second, second], axis=1).astype(BF16)


def finish_block(cols, data, total, low_stack, ortho_stack, err_out, q_out):
    summed = jnp.concatenate(three(total[:, cols]), axis=0)
    terms = nn(low_stack[...], summed)
    new_q = (terms[:RANK] + terms[RANK : 2 * RANK] + terms[2 * RANK :]) * (1.0 / DP)
    q_out[:, cols] = new_q
    first = new_q.astype(BF16)
    second = (new_q - first.astype(F32)).astype(BF16)
    approx = nn(ortho_stack[...], jnp.concatenate([first, second, first, second], axis=0))
    grad = data[:ROWS, cols].astype(F32)
    err = data[ROWS:, cols].astype(F32)
    err_out[:, cols] = (grad + err - approx).astype(BF16)


def exchange_kernel(
    grad_gate, err_gate, grad_up, err_up, q_gate, q_up,
    err_gate_out, q_gate_out, data_up, total_up, left, inverse,
    data_gate, total_gate, low_stack, ortho_stack,
    q_buf, p_acc, p_recv, p_stack, w_send, w_own, w_recv,
    a_recv0, a_recv1, a_recv2, a_sum0, a_sum1, a_sum2,
    b_recv0, b_recv1, b_recv2, c_recv0, c_recv1, c_recv2,
    g_part, g_recv, g_all, work, low,
    load_sem, p_send_sem, p_recv_sem, g_send_sem, g_recv_sem, w_send_sem, w_recv_sem,
):
    data = (data_gate, data_up)
    total = (total_gate, total_up)
    a_recv = (a_recv0, a_recv1, a_recv2)
    a_sum = (a_sum0, a_sum1, a_sum2)
    b_recv = (b_recv0, b_recv1, b_recv2)
    c_recv = (c_recv0, c_recv1, c_recv2)
    dp = lax.axis_index("dp")
    t = lax.axis_index("tensor")
    z, x = dp // 4, lax.rem(dp, 4)
    y, core = t // 2, lax.rem(t, 2)
    at = (x, y, z)
    one = dp // DP + 1

    def block(fn, *args):
        lax.fori_loop(0, one, lambda i, carry: (fn(*args), carry)[1], 0)

    def peer(axis, v):
        px, py, pz = (v if axis == i else at[i] for i in range(3))
        return (pz * 4 + px, py * 2 + core)

    def send(src, dst, send_sem, recv_sem, device):
        pltpu.make_async_remote_copy(
            src_ref=src, dst_ref=dst, send_sem=send_sem, recv_sem=recv_sem,
            device_id=device, device_id_type=MESH,
        ).start()

    def arrived(ref, sem):
        pltpu.make_async_copy(ref, ref, sem).wait()

    sources = ((q_gate, grad_gate, err_gate), (q_up, grad_up, err_up))

    def load(g, c, k):
        cols = pl.ds(pl.multiple_of(c * CHUNK, CHUNK), CHUNK)
        if k == 0:
            dst = q_buf.at[g, :, cols]
        else:
            dst = data[g].at[pl.ds((k - 1) * ROWS, ROWS), cols]
        return pltpu.make_async_copy(sources[g][k].at[:, cols], dst, load_sem.at[g, c, k])

    for g in range(2):
        for c in range(CHUNKS):
            for k in range(3):
                load(g, c, k).start()

    barrier = pltpu.get_barrier_semaphore()
    for d in range(1, DP):
        pl.semaphore_signal(
            barrier, inc=1, device_id=(lax.rem(dp + d, DP), t), device_id_type=MESH
        )
    for d in range(1, TENSOR):
        pl.semaphore_signal(
            barrier, inc=1, device_id=(dp, lax.rem(t + d, TENSOR)), device_id_type=MESH
        )

    def p_compute(g):
        p_acc[...] = jnp.zeros_like(p_acc)

        def step(c, carry):
            for k in range(3):
                load(g, c, k).wait()
            cols = pl.ds(pl.multiple_of(c * CHUNK, CHUNK), CHUNK)
            q3 = jnp.concatenate(three(q_buf[g, :, cols]), axis=0)
            p_acc[...] += nt(data[g][:, cols], q3)
            return carry

        lax.fori_loop(0, CHUNKS, step, 0)
        both = p_acc[:ROWS, :] + p_acc[ROWS:, :]
        turned = both.T
        summed = turned[:RANK] + turned[RANK : 2 * RANK] + turned[2 * RANK :]
        p_recv[g, 0, 0, x] = summed[: RANK // 2]
        p_recv[g, 0, 1, z] = summed[RANK // 2 :]

    def p_axis(step, h):
        return 0 if step == h else 2

    def p_start(g, step):
        for h in range(2):
            axis = p_axis(step, h)
            mine = p_recv.at[g, step, h, at[axis]]
            for d in range(1, 4):
                send(
                    mine, mine, p_send_sem.at[g, step, h], p_recv_sem.at[g, step, h],
                    peer(axis, lax.rem(at[axis] + d, 4)),
                )

    def p_sum(g, step, h):
        arrived(p_recv.at[g, step, h, pl.ds(0, 3)], p_recv_sem.at[g, step, h])
        return (
            p_recv[g, step, h, 0] + p_recv[g, step, h, 1]
            + p_recv[g, step, h, 2] + p_recv[g, step, h, 3]
        )

    def p_turn(g):
        for h in range(2):
            p_recv[g, 1, h, at[p_axis(1, h)]] = p_sum(g, 0, h)
        p_start(g, 1)

    def p_done(g):
        for h in range(2):
            left[g, h * (RANK // 2) : (h + 1) * (RANK // 2)] = p_sum(g, 1, h)
        p3 = jnp.concatenate(three(left[g]), axis=0)
        p_stack[g, :, :ROWS] = p3
        p_stack[g, :, ROWS:] = p3

    def w_block(g, dst, half, p):
        first, width = PARTS[p]
        start = pl.multiple_of(half * HALF + first, 128)

        for i in range(width // TILE):
            cols = pl.ds(pl.multiple_of(start + i * TILE, 128), TILE)
            prod = nn(p_stack[g], data[g][:, cols])
            dst[g, :, first + i * TILE : first + (i + 1) * TILE] = (
                prod[:RANK] + prod[RANK : 2 * RANK] + prod[2 * RANK :]
            )

    def sems(g, p, stage):
        return w_send_sem.at[g, p, stage], w_recv_sem.at[g, p, stage]

    def axes_of(g, p):
        first = (p + g) % 3
        return first, (first + 1) % 3, (first + 2) % 3

    def part_cols(p):
        return pl.ds(PARTS[p][0], PARTS[p][1])

    def total_block(g, p):
        a, _, _ = axes_of(g, p)
        first, width = PARTS[p]
        return total[g].at[
            pl.ds(pl.multiple_of(16 * at[a], 16), 16),
            pl.ds(pl.multiple_of(core * HALF + first, 128), width),
        ]

    def total_leaf(g, p):
        a, b, _ = axes_of(g, p)
        first, width = PARTS[p]
        row = 16 * at[a] + 8 * (at[b] // 2)
        col = core * HALF + first + (width // 2) * lax.rem(at[b], 2)
        return total[g].at[
            pl.ds(pl.multiple_of(row, 8), 8), pl.ds(pl.multiple_of(col, 128), width // 2)
        ]

    def core_start(g):
        def step(p):
            w_block(g, w_send, 1 - core, p)
            send(
                w_send.at[g, :, part_cols(p)], w_recv.at[g, :, part_cols(p)],
                *sems(g, p, CORE_SUM), (dp, y * 2 + 1 - core),
            )

        for p in range(3):
            block(step, p)

    def w_rest(g):
        for p in range(3):
            w_block(g, w_own, core, p)

    def a_start(g):
        def step(p):
            cols = part_cols(p)
            arrived(w_recv.at[g, :, cols], w_recv_sem.at[g, p, CORE_SUM])
            w_own[g, :, cols] += w_recv[g, :, cols]
            a, _, _ = axes_of(g, p)
            for d in range(1, 4):
                v = lax.rem(at[a] + d, 4)
                send(
                    w_own.at[g, pl.ds(pl.multiple_of(16 * v, 16), 16), cols],
                    a_recv[p].at[g, d - 1],
                    *sems(g, p, A_SUM), peer(a, v),
                )

        for p in range(3):
            block(step, p)

    def b_start(g):
        def step(p):
            a, b, _ = axes_of(g, p)
            first, width = PARTS[p]
            arrived(a_recv[p].at[g], w_recv_sem.at[g, p, A_SUM])
            a_sum[p][g] = (
                w_own[g, pl.ds(pl.multiple_of(16 * at[a], 16), 16), part_cols(p)]
                + a_recv[p][g, 0] + a_recv[p][g, 1] + a_recv[p][g, 2]
            )
            for d in range(1, 4):
                v = lax.rem(at[b] + d, 4)
                send(
                    a_sum[p].at[g, leaf_rows(v), leaf_cols(v, width)], b_recv[p].at[g, d - 1],
                    *sems(g, p, B_SUM), peer(b, v),
                )

        for p in range(3):
            block(step, p)

    def leaf_rows(v):
        return pl.ds(pl.multiple_of(8 * (v // 2), 8), 8)

    def leaf_cols(v, width):
        return pl.ds(pl.multiple_of((width // 2) * lax.rem(v, 2), 128), width // 2)

    def c_start(g):
        def step(p):
            _, b, c = axes_of(g, p)
            first, width = PARTS[p]
            arrived(b_recv[p].at[g], w_recv_sem.at[g, p, B_SUM])
            c_recv[p][g, at[c]] = (
                a_sum[p][g, leaf_rows(at[b]), leaf_cols(at[b], width)]
                + b_recv[p][g, 0] + b_recv[p][g, 1] + b_recv[p][g, 2]
            )
            for d in range(1, 4):
                send(
                    c_recv[p].at[g, at[c]], c_recv[p].at[g, at[c]],
                    *sems(g, p, C_SUM), peer(c, lax.rem(at[c] + d, 4)),
                )

        for p in range(3):
            block(step, p)

    def b_all_start(g):
        def step(p):
            _, b, _ = axes_of(g, p)
            arrived(c_recv[p].at[g, pl.ds(0, 3)], w_recv_sem.at[g, p, C_SUM])
            leaf = total_leaf(g, p)
            leaf[...] = c_recv[p][g, 0] + c_recv[p][g, 1] + c_recv[p][g, 2] + c_recv[p][g, 3]
            for d in range(1, 4):
                send(leaf, leaf, *sems(g, p, B_ALL), peer(b, lax.rem(at[b] + d, 4)))

        for p in range(3):
            block(step, p)

    def a_all_start(g):
        def step(p):
            a, _, _ = axes_of(g, p)
            arrived(b_recv[p].at[g], w_recv_sem.at[g, p, B_ALL])
            block = total_block(g, p)
            for d in range(1, 4):
                send(block, block, *sems(g, p, A_ALL), peer(a, lax.rem(at[a] + d, 4)))

        for p in range(3):
            block(step, p)

    def core_all_start(g):
        def step(p):
            first, width = PARTS[p]
            arrived(a_recv[p].at[g], w_recv_sem.at[g, p, A_ALL])
            part = total[g].at[:, pl.ds(pl.multiple_of(core * HALF + first, 128), width)]
            send(part, part, *sems(g, p, CORE_ALL), (dp, y * 2 + 1 - core))

        for p in range(3):
            block(step, p)

    def core_all_done(g):
        for p in range(3):
            arrived(w_recv.at[g, :, part_cols(p)], w_recv_sem.at[g, p, CORE_ALL])

    member = lax.rem(dp, 8)
    mine = pl.ds(pl.multiple_of(8 * member, 8), 8)

    def gram_start():
        for g in range(2):
            g_part[:, g * RANK : (g + 1) * RANK] = nt(left[g], left[g], HP)
        for d in range(1, TENSOR):
            send(
                g_part.at[mine, :], g_recv.at[t],
                g_send_sem.at[0], g_recv_sem.at[0], (dp, lax.rem(t + d, TENSOR)),
            )
        g_recv[t] = g_part[mine, :]

    def gram_all_start():
        arrived(g_recv.at[pl.ds(0, 7)], g_recv_sem.at[0])
        summed = g_recv[0]
        for i in range(1, TENSOR):
            summed = summed + g_recv[i]
        g_all[mine, :] = summed
        for d in range(1, 8):
            other = 8 * (dp // 8) + lax.rem(member + d, 8)
            send(
                g_all.at[mine, :], g_all.at[mine, :],
                g_send_sem.at[1], g_recv_sem.at[1], (other, t),
            )

    lane = lax.broadcasted_iota(jnp.int32, (RANK, 2 * RANK), 1)
    row = lax.broadcasted_iota(jnp.int32, (RANK, 2 * RANK), 0)
    lane_one = lax.broadcasted_iota(jnp.int32, (1, 2 * RANK), 1)

    def gram_done():
        arrived(g_recv.at[pl.ds(0, 7)], g_recv_sem.at[1])
        work[...] = g_all[...]
        low[...] = jnp.where(lax.rem(lane, RANK) == row, 1.0, 0.0).astype(F32)

    def halves(value, lanes, column):
        gate = jnp.sum(jnp.where(lanes == column, value, 0.0), axis=1, keepdims=True)
        up = jnp.sum(jnp.where(lanes == column + RANK, value, 0.0), axis=1, keepdims=True)
        return jnp.where(lanes < RANK, gate, up)

    def eliminate(first, last):
        def step(j, carry):
            value = work[...]
            pivot_row = work[pl.ds(j, 1), :]
            low_row = low[pl.ds(j, 1), :]
            scale = 1.0 / halves(pivot_row, lane_one, j)
            factor = jnp.where(row > j, halves(value, lane, j) * scale, 0.0)
            work[...] = value - factor * pivot_row
            low[...] = low[...] - factor * low_row
            return carry

        lax.fori_loop(first, last, step, 0)

    def inverse_done():
        value = work[...]
        on = lax.rem(lane, RANK) == row
        gate = jnp.sum(jnp.where(on & (lane < RANK), value, 0.0), axis=1, keepdims=True)
        up = jnp.sum(jnp.where(on & (lane >= RANK), value, 0.0), axis=1, keepdims=True)
        diagonal = jnp.where(lane < RANK, gate, up)
        inverse[...] = low[...] / jnp.sqrt(diagonal)

    def finish_gate():
        finish_stacks(inverse[:, :RANK], left[0], low_stack, ortho_stack)
        for i in range(BLOCKS):
            finish_block(
                slice(i * BLOCK, (i + 1) * BLOCK), data_gate, total_gate, low_stack, ortho_stack,
                err_gate_out, q_gate_out,
            )

    p_compute(0)
    pl.semaphore_wait(barrier, DP + TENSOR - 2)
    p_start(0, 0)
    p_compute(1)
    p_start(1, 0)
    block(p_turn, 0)
    block(p_turn, 1)
    block(p_done, 0)
    core_start(0)
    block(w_rest, 0)
    a_start(0)
    block(p_done, 1)
    core_start(1)
    block(w_rest, 1)
    block(gram_start)
    a_start(1)
    b_start(0)
    block(gram_all_start)
    b_start(1)
    c_start(0)
    block(gram_done)
    eliminate(0, 20)
    c_start(1)
    b_all_start(0)
    eliminate(20, 42)
    b_all_start(1)
    a_all_start(0)
    eliminate(42, RANK)
    block(inverse_done)
    a_all_start(1)
    core_all_start(0)
    core_all_start(1)
    core_all_done(0)
    block(finish_gate)
    core_all_done(1)

    for g in range(2):
        for step in range(2):
            for h in range(2):
                arrived(p_recv.at[g, step, h, pl.ds(0, 3)], p_send_sem.at[g, step, h])
        for p in range(3):
            cols = part_cols(p)
            arrived(w_recv.at[g, :, cols], w_send_sem.at[g, p, CORE_SUM])
            arrived(w_recv.at[g, :, cols], w_send_sem.at[g, p, CORE_ALL])
            for stage in (A_SUM, A_ALL):
                arrived(a_recv[p].at[g], w_send_sem.at[g, p, stage])
            for stage in (B_SUM, C_SUM, B_ALL):
                arrived(b_recv[p].at[g], w_send_sem.at[g, p, stage])
    for phase in range(2):
        arrived(g_recv.at[pl.ds(0, 7)], g_send_sem.at[phase])


def finish_kernel(
    err_gate, q_gate, data, total, left, inverse,
    new_err_gate, new_err_up, new_q_gate, new_q_up,
    err_up, q_up, low_stack, ortho_stack, sem,
):
    gate = (
        pltpu.make_async_copy(err_gate, new_err_gate, sem.at[0]),
        pltpu.make_async_copy(q_gate, new_q_gate, sem.at[1]),
    )
    for copy in gate:
        copy.start()
    finish_stacks(inverse[:, RANK:], left[1], low_stack, ortho_stack)

    def copies(i):
        cols = pl.ds(pl.multiple_of(i * BLOCK, BLOCK), BLOCK)
        return (
            pltpu.make_async_copy(err_up.at[:, cols], new_err_up.at[:, cols], sem.at[2]),
            pltpu.make_async_copy(q_up.at[:, cols], new_q_up.at[:, cols], sem.at[3]),
        )

    def step(i, carry):
        finish_block(
            pl.ds(pl.multiple_of(i * BLOCK, BLOCK), BLOCK), data, total, low_stack, ortho_stack,
            err_up, q_up,
        )
        for copy in copies(i):
            copy.start()
        return carry

    lax.fori_loop(0, BLOCKS, step, 0)
    for copy in gate:
        copy.wait()
    pltpu.make_async_copy(err_up, new_err_up, sem.at[2]).wait()
    pltpu.make_async_copy(q_up, new_q_up, sem.at[3]).wait()


def body(grad_gate, grad_up, err_gate, err_up, q_gate, q_up):
    def part_scratch(*lead):
        def of(divide, rows):
            return [pltpu.VMEM(lead + (rows, width // divide), F32) for _, width in PARTS]

        return of

    made = pl.pallas_call(
        exchange_kernel,
        out_shape=(
            pltpu.VMEM((ROWS, D), BF16),
            pltpu.VMEM((RANK, D), F32),
            pltpu.VMEM((2 * ROWS, D), BF16),
            pltpu.VMEM((RANK, D), F32),
            pltpu.VMEM((2, RANK, ROWS), F32),
            pltpu.VMEM((RANK, 2 * RANK), F32),
        ),
        in_specs=[pl.BlockSpec(memory_space=pl.ANY)] * 6,
        out_specs=[pl.BlockSpec(memory_space=pltpu.VMEM)] * 6,
        scratch_shapes=[
            pltpu.VMEM((2 * ROWS, D), BF16),
            pltpu.VMEM((RANK, D), F32),
            pltpu.VMEM((3 * RANK, 3 * RANK), BF16),
            pltpu.VMEM((ROWS, 4 * RANK), BF16),
            pltpu.VMEM((2, RANK, D), F32),
            pltpu.VMEM((2 * ROWS, 3 * RANK), F32),
            pltpu.VMEM((2, 2, 2, 4, RANK // 2, ROWS), F32),
            pltpu.VMEM((2, 3 * RANK, 2 * ROWS), BF16),
            pltpu.VMEM((2, RANK, HALF), F32),
            pltpu.VMEM((2, RANK, HALF), F32),
            pltpu.VMEM((2, RANK, HALF), F32),
            *part_scratch(2, 3)(1, 16),
            *part_scratch(2)(1, 16),
            *part_scratch(2, 3)(2, 8),
            *part_scratch(2, 4)(2, 8),
            pltpu.VMEM((RANK, 2 * RANK), F32),
            pltpu.VMEM((TENSOR, 8, 2 * RANK), F32),
            pltpu.VMEM((RANK, 2 * RANK), F32),
            pltpu.VMEM((RANK, 2 * RANK), F32),
            pltpu.VMEM((RANK, 2 * RANK), F32),
            pltpu.SemaphoreType.DMA((2, CHUNKS, 3)),
            pltpu.SemaphoreType.DMA((2, 2, 2)),
            pltpu.SemaphoreType.DMA((2, 2, 2)),
            pltpu.SemaphoreType.DMA((2,)),
            pltpu.SemaphoreType.DMA((2,)),
            pltpu.SemaphoreType.DMA((2, 3, STAGES)),
            pltpu.SemaphoreType.DMA((2, 3, STAGES)),
        ],
        compiler_params=pltpu.CompilerParams(
            collective_id=0, has_side_effects=True, vmem_limit_bytes=32 * 2**20
        ),
        name="exchange",
    )(
        *(
            pltpu.with_memory_space_constraint(v, pltpu.HBM)
            for v in (
                grad_gate.reshape(ROWS, D), err_gate.reshape(ROWS, D),
                grad_up.reshape(ROWS, D), err_up.reshape(ROWS, D), q_gate.T, q_up.T,
            )
        )
    )
    held = [pltpu.with_memory_space_constraint(v, pltpu.VMEM) for v in made]
    new_err_gate, new_err_up, new_q_gate, new_q_up = pl.pallas_call(
        finish_kernel,
        out_shape=(
            jax.ShapeDtypeStruct((ROWS, D), BF16),
            jax.ShapeDtypeStruct((ROWS, D), BF16),
            jax.ShapeDtypeStruct((RANK, D), F32),
            jax.ShapeDtypeStruct((RANK, D), F32),
        ),
        in_specs=[pl.BlockSpec(memory_space=pltpu.VMEM)] * 6,
        out_specs=[pl.BlockSpec(memory_space=pl.ANY)] * 4,
        scratch_shapes=[
            pltpu.VMEM((ROWS, D), BF16),
            pltpu.VMEM((RANK, D), F32),
            pltpu.VMEM((3 * RANK, 3 * RANK), BF16),
            pltpu.VMEM((ROWS, 4 * RANK), BF16),
            pltpu.SemaphoreType.DMA((4,)),
        ],
        compiler_params=pltpu.CompilerParams(vmem_limit_bytes=12 * 2**20),
        name="finish",
    )(*held)
    return (
        new_err_gate.reshape(1, ROWS, D),
        new_err_up.reshape(1, ROWS, D),
        new_q_gate.T,
        new_q_up.T,
    )


def solution(mesh):
    placed = P("dp", "tensor", None)
    return jax.shard_map(
        body,
        mesh=mesh,
        in_specs=(placed, placed, placed, placed, P(), P()),
        out_specs=(placed, placed, P(), P()),
        check_vma=False,
    )
```

```python
import functools

import jax
import jax.numpy as jnp
from jax import lax
from jax.experimental import pallas as pl
from jax.experimental.pallas import tpu as pltpu
from jax.sharding import PartitionSpec as P

MESH = pl.DeviceIdType.MESH
F32 = jnp.float32
BF16 = jnp.bfloat16
HP = lax.Precision.HIGHEST

DP = 16
TENSOR = 8
D = 7168
ROWS = 256
RANK = 64
HALF = D // 2
CHUNKS = 4
CHUNK = D // CHUNKS
TILE = 256
PARTS = ((0, 1280), (1280, 1280), (2560, 1024))
BLOCKS = 4
BLOCK = D // BLOCKS
STAGES = 8
CORE_SUM, A_SUM, B_SUM, C_SUM, B_ALL, A_ALL, CORE_ALL, A_FAR = range(STAGES)


SUMS = (CORE_SUM, A_SUM, B_SUM, C_SUM, B_ALL)


def three(value):
    first = value.astype(BF16)
    rest = value - first.astype(F32)
    second = rest.astype(BF16)
    third = (rest - second.astype(F32)).astype(BF16)
    return first, second, third


def nt(left, right, precision=None):
    return lax.dot_general(
        left, right, (((1,), (1,)), ((), ())), precision=precision, preferred_element_type=F32
    )


def nn(left, right, precision=None):
    return jnp.dot(left, right, precision=precision, preferred_element_type=F32)


def finish_stacks(low, left, low_stack, ortho_stack):
    column = jnp.concatenate(three(low), axis=0)
    low_stack[...] = jnp.concatenate([column, column, column], axis=1)
    ortho = nn(low, left, HP).T
    first = ortho.astype(BF16).astype(F32)
    second = ortho - first
    ortho_stack[...] = jnp.concatenate([first, first, second, second], axis=1).astype(BF16)


def finish_block(cols, data, total, low_stack, ortho_stack, err_out, q_out):
    summed = jnp.concatenate(three(total[:, cols]), axis=0)
    terms = nn(low_stack[...], summed)
    new_q = (terms[:RANK] + terms[RANK : 2 * RANK] + terms[2 * RANK :]) * (1.0 / DP)
    q_out[:, cols] = new_q
    first = new_q.astype(BF16)
    second = (new_q - first.astype(F32)).astype(BF16)
    approx = nn(ortho_stack[...], jnp.concatenate([first, second, first, second], axis=0))
    grad = data[:ROWS, cols].astype(F32)
    err = data[ROWS:, cols].astype(F32)
    err_out[:, cols] = (grad + err - approx).astype(BF16)


def exchange_kernel(
    grad_gate, err_gate, grad_up, err_up, q_gate, q_up,
    err_gate_out, q_gate_out, data_up, total_up, left, inverse,
    data_gate, total_gate, low_stack, ortho_stack,
    q_buf, p_acc, p_recv, p_stack, w_send, w_own, w_recv,
    a_recv0, a_recv1, a_recv2, a_sum0, a_sum1, a_sum2,
    b_recv0, b_recv1, b_recv2, c_recv0, c_recv1, c_recv2,
    g_part, g_recv, g_all, work, low,
    load_sem, p_send_sem, p_recv_sem, g_send_sem, g_recv_sem, w_send_sem, w_recv_sem,
):
    data = (data_gate, data_up)
    total = (total_gate, total_up)
    a_recv = (a_recv0, a_recv1, a_recv2)
    a_sum = (a_sum0, a_sum1, a_sum2)
    b_recv = (b_recv0, b_recv1, b_recv2)
    c_recv = (c_recv0, c_recv1, c_recv2)
    dp = lax.axis_index("dp")
    t = lax.axis_index("tensor")
    z, x = dp // 4, lax.rem(dp, 4)
    y, core = t // 2, lax.rem(t, 2)
    at = (x, y, z)
    one = dp // DP + 1

    def block(fn, *args):
        lax.fori_loop(0, one, lambda i, carry: (fn(*args), carry)[1], 0)

    def peer(axis, v):
        px, py, pz = (v if axis == i else at[i] for i in range(3))
        return (pz * 4 + px, py * 2 + core)

    def send(src, dst, send_sem, recv_sem, device):
        pltpu.make_async_remote_copy(
            src_ref=src, dst_ref=dst, send_sem=send_sem, recv_sem=recv_sem,
            device_id=device, device_id_type=MESH,
        ).start()

    def arrived(ref, sem):
        pltpu.make_async_copy(ref, ref, sem).wait()

    sources = ((q_gate, grad_gate, err_gate), (q_up, grad_up, err_up))

    def load(g, c, k):
        cols = pl.ds(pl.multiple_of(c * CHUNK, CHUNK), CHUNK)
        if k == 0:
            dst = q_buf.at[g, :, cols]
        else:
            dst = data[g].at[pl.ds((k - 1) * ROWS, ROWS), cols]
        return pltpu.make_async_copy(sources[g][k].at[:, cols], dst, load_sem.at[g, c, k])

    for g in range(2):
        for c in range(CHUNKS):
            for k in range(3):
                load(g, c, k).start()

    barrier = pltpu.get_barrier_semaphore()
    for d in range(1, DP):
        pl.semaphore_signal(
            barrier, inc=1, device_id=(lax.rem(dp + d, DP), t), device_id_type=MESH
        )
    for d in range(1, TENSOR):
        pl.semaphore_signal(
            barrier, inc=1, device_id=(dp, lax.rem(t + d, TENSOR)), device_id_type=MESH
        )

    def p_compute(g):
        p_acc[...] = jnp.zeros_like(p_acc)

        def step(c, carry):
            for k in range(3):
                load(g, c, k).wait()
            cols = pl.ds(pl.multiple_of(c * CHUNK, CHUNK), CHUNK)
            q3 = jnp.concatenate(three(q_buf[g, :, cols]), axis=0)
            p_acc[...] += nt(data[g][:, cols], q3)
            return carry

        lax.fori_loop(0, CHUNKS, step, 0)
        both = p_acc[:ROWS, :] + p_acc[ROWS:, :]
        turned = both.T
        summed = turned[:RANK] + turned[RANK : 2 * RANK] + turned[2 * RANK :]
        p_recv[g, 0, 0, x] = summed[: RANK // 2]
        p_recv[g, 0, 1, z] = summed[RANK // 2 :]

    def p_axis(step, h):
        return 0 if step == h else 2

    def p_start(g, step):
        for h in range(2):
            axis = p_axis(step, h)
            mine = p_recv.at[g, step, h, at[axis]]
            for d in range(1, 4):
                send(
                    mine, mine, p_send_sem.at[g, step, h], p_recv_sem.at[g, step, h],
                    peer(axis, lax.rem(at[axis] + d, 4)),
                )

    def p_sum(g, step, h):
        arrived(p_recv.at[g, step, h, pl.ds(0, 3)], p_recv_sem.at[g, step, h])
        return (
            p_recv[g, step, h, 0] + p_recv[g, step, h, 1]
            + p_recv[g, step, h, 2] + p_recv[g, step, h, 3]
        )

    def p_turn(g):
        for h in range(2):
            p_recv[g, 1, h, at[p_axis(1, h)]] = p_sum(g, 0, h)
        p_start(g, 1)

    def p_done(g):
        for h in range(2):
            left[g, h * (RANK // 2) : (h + 1) * (RANK // 2)] = p_sum(g, 1, h)
        p3 = jnp.concatenate(three(left[g]), axis=0)
        p_stack[g, :, :ROWS] = p3
        p_stack[g, :, ROWS:] = p3

    def w_block(g, dst, half, p):
        first, width = PARTS[p]
        start = pl.multiple_of(half * HALF + first, 128)

        for i in range(width // TILE):
            cols = pl.ds(pl.multiple_of(start + i * TILE, 128), TILE)
            prod = nn(p_stack[g], data[g][:, cols])
            dst[g, :, first + i * TILE : first + (i + 1) * TILE] = (
                prod[:RANK] + prod[RANK : 2 * RANK] + prod[2 * RANK :]
            )

    def sems(g, p, stage):
        return w_send_sem.at[g, p, stage], w_recv_sem.at[g, p, stage]

    def axes_of(g, p):
        first = (p + g) % 3
        return first, (first + 1) % 3, (first + 2) % 3

    def part_cols(p):
        return pl.ds(PARTS[p][0], PARTS[p][1])

    def total_block(g, p, v):
        first, width = PARTS[p]
        return total[g].at[
            pl.ds(pl.multiple_of(16 * v, 16), 16),
            pl.ds(pl.multiple_of(core * HALF + first, 128), width),
        ]

    def total_leaf(g, p):
        a, b, _ = axes_of(g, p)
        first, width = PARTS[p]
        row = 16 * at[a] + 8 * (at[b] // 2)
        col = core * HALF + first + (width // 2) * lax.rem(at[b], 2)
        return total[g].at[
            pl.ds(pl.multiple_of(row, 8), 8), pl.ds(pl.multiple_of(col, 128), width // 2)
        ]

    def core_start(g):
        def step(p):
            w_block(g, w_send, 1 - core, p)
            send(
                w_send.at[g, :, part_cols(p)], w_recv.at[g, :, part_cols(p)],
                *sems(g, p, CORE_SUM), (dp, y * 2 + 1 - core),
            )

        for p in range(3):
            block(step, p)

    def a_start(g):
        def step(p):
            cols = part_cols(p)
            arrived(w_recv.at[g, :, cols], w_recv_sem.at[g, p, CORE_SUM])
            w_own[g, :, cols] += w_recv[g, :, cols]
            a, _, _ = axes_of(g, p)
            for d in range(1, 4):
                v = lax.rem(at[a] + d, 4)
                send(
                    w_own.at[g, pl.ds(pl.multiple_of(16 * v, 16), 16), cols],
                    a_recv[p].at[g, d - 1],
                    *sems(g, p, A_SUM), peer(a, v),
                )

        for p in range(3):
            block(w_block, g, w_own, core, p)
            block(step, p)

    def b_start(g):
        def step(p):
            a, b, _ = axes_of(g, p)
            first, width = PARTS[p]
            arrived(a_recv[p].at[g], w_recv_sem.at[g, p, A_SUM])
            a_sum[p][g] = (
                w_own[g, pl.ds(pl.multiple_of(16 * at[a], 16), 16), part_cols(p)]
                + a_recv[p][g, 0] + a_recv[p][g, 1] + a_recv[p][g, 2]
            )
            for d in range(1, 4):
                v = lax.rem(at[b] + d, 4)
                send(
                    a_sum[p].at[g, leaf_rows(v), leaf_cols(v, width)], b_recv[p].at[g, d - 1],
                    *sems(g, p, B_SUM), peer(b, v),
                )

        for p in range(3):
            block(step, p)

    def leaf_rows(v):
        return pl.ds(pl.multiple_of(8 * (v // 2), 8), 8)

    def leaf_cols(v, width):
        return pl.ds(pl.multiple_of((width // 2) * lax.rem(v, 2), 128), width // 2)

    def c_start(g):
        def step(p):
            _, b, c = axes_of(g, p)
            first, width = PARTS[p]
            arrived(b_recv[p].at[g], w_recv_sem.at[g, p, B_SUM])
            c_recv[p][g, at[c]] = (
                a_sum[p][g, leaf_rows(at[b]), leaf_cols(at[b], width)]
                + b_recv[p][g, 0] + b_recv[p][g, 1] + b_recv[p][g, 2]
            )
            for d in range(1, 4):
                send(
                    c_recv[p].at[g, at[c]], c_recv[p].at[g, at[c]],
                    *sems(g, p, C_SUM), peer(c, lax.rem(at[c] + d, 4)),
                )

        for p in range(3):
            block(step, p)

    def b_all_start(g):
        def step(p):
            _, b, _ = axes_of(g, p)
            arrived(c_recv[p].at[g, pl.ds(0, 3)], w_recv_sem.at[g, p, C_SUM])
            leaf = total_leaf(g, p)
            leaf[...] = c_recv[p][g, 0] + c_recv[p][g, 1] + c_recv[p][g, 2] + c_recv[p][g, 3]
            for d in range(1, 4):
                send(leaf, leaf, *sems(g, p, B_ALL), peer(b, lax.rem(at[b] + d, 4)))

        for p in range(3):
            block(step, p)

    def a_all_start(g):
        def step(p):
            a, _, _ = axes_of(g, p)
            arrived(b_recv[p].at[g], w_recv_sem.at[g, p, B_ALL])
            mine = total_block(g, p, at[a])
            for d in (1, 3, 2):
                send(
                    mine, mine, w_send_sem.at[g, p, A_ALL],
                    w_recv_sem.at[g, p, A_FAR if d == 2 else A_ALL],
                    peer(a, lax.rem(at[a] + d, 4)),
                )
            send(mine, mine, *sems(g, p, CORE_ALL), (dp, y * 2 + 1 - core))

        for p in range(3):
            block(step, p)

    def core_all_start(g, far):
        def step(p):
            a, _, _ = axes_of(g, p)
            if far:
                arrived(a_recv[p].at[g, 0], w_recv_sem.at[g, p, A_FAR])
            else:
                arrived(a_recv[p].at[g, pl.ds(0, 2)], w_recv_sem.at[g, p, A_ALL])
            for d in (2,) if far else (1, 3):
                block_of = total_block(g, p, lax.rem(at[a] + d, 4))
                send(block_of, block_of, *sems(g, p, CORE_ALL), (dp, y * 2 + 1 - core))

        for p in range(3):
            block(step, p)

    def core_all_done(g):
        for p in range(3):
            arrived(w_recv.at[g, :, part_cols(p)], w_recv_sem.at[g, p, CORE_ALL])

    member = lax.rem(dp, 8)
    mine = pl.ds(pl.multiple_of(8 * member, 8), 8)

    def gram_start():
        for g in range(2):
            g_part[:, g * RANK : (g + 1) * RANK] = nt(left[g], left[g], HP)
        for d in range(1, TENSOR):
            send(
                g_part.at[mine, :], g_recv.at[t],
                g_send_sem.at[0], g_recv_sem.at[0], (dp, lax.rem(t + d, TENSOR)),
            )
        g_recv[t] = g_part[mine, :]

    def gram_all_start():
        arrived(g_recv.at[pl.ds(0, 7)], g_recv_sem.at[0])
        summed = g_recv[0]
        for i in range(1, TENSOR):
            summed = summed + g_recv[i]
        g_all[mine, :] = summed
        for d in range(1, 8):
            other = 8 * (dp // 8) + lax.rem(member + d, 8)
            send(
                g_all.at[mine, :], g_all.at[mine, :],
                g_send_sem.at[1], g_recv_sem.at[1], (other, t),
            )

    lane = lax.broadcasted_iota(jnp.int32, (RANK, 2 * RANK), 1)
    row = lax.broadcasted_iota(jnp.int32, (RANK, 2 * RANK), 0)
    lane_one = lax.broadcasted_iota(jnp.int32, (1, 2 * RANK), 1)

    def gram_done():
        arrived(g_recv.at[pl.ds(0, 7)], g_recv_sem.at[1])
        work[...] = g_all[...]
        low[...] = jnp.where(lax.rem(lane, RANK) == row, 1.0, 0.0).astype(F32)

    def halves(value, lanes, column):
        gate = jnp.sum(jnp.where(lanes == column, value, 0.0), axis=1, keepdims=True)
        up = jnp.sum(jnp.where(lanes == column + RANK, value, 0.0), axis=1, keepdims=True)
        return jnp.where(lanes < RANK, gate, up)

    def eliminate(first, last):
        def step(j, carry):
            value = work[...]
            pivot_row = work[pl.ds(j, 1), :]
            low_row = low[pl.ds(j, 1), :]
            scale = 1.0 / halves(pivot_row, lane_one, j)
            factor = jnp.where(row > j, halves(value, lane, j) * scale, 0.0)
            work[...] = value - factor * pivot_row
            low[...] = low[...] - factor * low_row
            return carry

        lax.fori_loop(first, last, step, 0)

    def inverse_done():
        value = work[...]
        on = lax.rem(lane, RANK) == row
        gate = jnp.sum(jnp.where(on & (lane < RANK), value, 0.0), axis=1, keepdims=True)
        up = jnp.sum(jnp.where(on & (lane >= RANK), value, 0.0), axis=1, keepdims=True)
        diagonal = jnp.where(lane < RANK, gate, up)
        inverse[...] = low[...] / jnp.sqrt(diagonal)

    def finish_gate():
        finish_stacks(inverse[:, :RANK], left[0], low_stack, ortho_stack)
        for i in range(BLOCKS):
            finish_block(
                slice(i * BLOCK, (i + 1) * BLOCK), data_gate, total_gate, low_stack, ortho_stack,
                err_gate_out, q_gate_out,
            )

    def p_sent():
        for g in range(2):
            for step in range(2):
                for h in range(2):
                    arrived(p_recv.at[g, step, h, pl.ds(0, 3)], p_send_sem.at[g, step, h])
        for phase in range(2):
            arrived(g_recv.at[pl.ds(0, 7)], g_send_sem.at[phase])

    def w_sent(g, stages):
        for p in range(3):
            half = w_recv.at[g, :, part_cols(p)]
            refs = {CORE_SUM: half, CORE_ALL: half, A_SUM: a_recv[p].at[g], A_ALL: a_recv[p].at[g]}
            for stage in stages:
                arrived(refs.get(stage, b_recv[p].at[g]), w_send_sem.at[g, p, stage])

    p_compute(0)
    pl.semaphore_wait(barrier, DP + TENSOR - 2)
    p_start(0, 0)
    p_compute(1)
    p_start(1, 0)
    block(p_turn, 0)
    block(p_turn, 1)
    block(p_done, 0)
    core_start(0)
    a_start(0)
    block(p_done, 1)
    core_start(1)
    a_start(1)
    block(gram_start)
    b_start(0)
    block(gram_all_start)
    b_start(1)
    c_start(0)
    block(gram_done)
    eliminate(0, 20)
    c_start(1)
    b_all_start(0)
    eliminate(20, 42)
    b_all_start(1)
    a_all_start(0)
    eliminate(42, 50)
    a_all_start(1)
    eliminate(50, RANK)
    block(inverse_done)
    core_all_start(0, False)
    core_all_start(0, True)
    block(p_sent)
    block(w_sent, 0, SUMS)
    block(w_sent, 1, SUMS)
    core_all_start(1, False)
    core_all_done(0)
    block(finish_gate)
    block(w_sent, 0, (A_ALL, CORE_ALL))
    core_all_start(1, True)
    core_all_done(1)
    block(w_sent, 1, (A_ALL, CORE_ALL))


def finish_kernel(
    err_gate, q_gate, data, total, left, inverse,
    new_err_gate, new_err_up, new_q_gate, new_q_up,
    err_up, q_up, low_stack, ortho_stack, sem,
):
    gate = (
        pltpu.make_async_copy(err_gate, new_err_gate, sem.at[0]),
        pltpu.make_async_copy(q_gate, new_q_gate, sem.at[1]),
    )
    for copy in gate:
        copy.start()
    finish_stacks(inverse[:, RANK:], left[1], low_stack, ortho_stack)

    def copies(i):
        cols = pl.ds(pl.multiple_of(i * BLOCK, BLOCK), BLOCK)
        return (
            pltpu.make_async_copy(err_up.at[:, cols], new_err_up.at[:, cols], sem.at[2]),
            pltpu.make_async_copy(q_up.at[:, cols], new_q_up.at[:, cols], sem.at[3]),
        )

    def step(i, carry):
        finish_block(
            pl.ds(pl.multiple_of(i * BLOCK, BLOCK), BLOCK), data, total, low_stack, ortho_stack,
            err_up, q_up,
        )
        for copy in copies(i):
            copy.start()
        return carry

    lax.fori_loop(0, BLOCKS, step, 0)
    for copy in gate:
        copy.wait()
    pltpu.make_async_copy(err_up, new_err_up, sem.at[2]).wait()
    pltpu.make_async_copy(q_up, new_q_up, sem.at[3]).wait()


def body(grad_gate, grad_up, err_gate, err_up, q_gate, q_up):
    def part_scratch(*lead):
        def of(divide, rows):
            return [pltpu.VMEM(lead + (rows, width // divide), F32) for _, width in PARTS]

        return of

    made = pl.pallas_call(
        exchange_kernel,
        out_shape=(
            pltpu.VMEM((ROWS, D), BF16),
            pltpu.VMEM((RANK, D), F32),
            pltpu.VMEM((2 * ROWS, D), BF16),
            pltpu.VMEM((RANK, D), F32),
            pltpu.VMEM((2, RANK, ROWS), F32),
            pltpu.VMEM((RANK, 2 * RANK), F32),
        ),
        in_specs=[pl.BlockSpec(memory_space=pl.ANY)] * 6,
        out_specs=[pl.BlockSpec(memory_space=pltpu.VMEM)] * 6,
        scratch_shapes=[
            pltpu.VMEM((2 * ROWS, D), BF16),
            pltpu.VMEM((RANK, D), F32),
            pltpu.VMEM((3 * RANK, 3 * RANK), BF16),
            pltpu.VMEM((ROWS, 4 * RANK), BF16),
            pltpu.VMEM((2, RANK, D), F32),
            pltpu.VMEM((2 * ROWS, 3 * RANK), F32),
            pltpu.VMEM((2, 2, 2, 4, RANK // 2, ROWS), F32),
            pltpu.VMEM((2, 3 * RANK, 2 * ROWS), BF16),
            pltpu.VMEM((2, RANK, HALF), F32),
            pltpu.VMEM((2, RANK, HALF), F32),
            pltpu.VMEM((2, RANK, HALF), F32),
            *part_scratch(2, 3)(1, 16),
            *part_scratch(2)(1, 16),
            *part_scratch(2, 3)(2, 8),
            *part_scratch(2, 4)(2, 8),
            pltpu.VMEM((RANK, 2 * RANK), F32),
            pltpu.VMEM((TENSOR, 8, 2 * RANK), F32),
            pltpu.VMEM((RANK, 2 * RANK), F32),
            pltpu.VMEM((RANK, 2 * RANK), F32),
            pltpu.VMEM((RANK, 2 * RANK), F32),
            pltpu.SemaphoreType.DMA((2, CHUNKS, 3)),
            pltpu.SemaphoreType.DMA((2, 2, 2)),
            pltpu.SemaphoreType.DMA((2, 2, 2)),
            pltpu.SemaphoreType.DMA((2,)),
            pltpu.SemaphoreType.DMA((2,)),
            pltpu.SemaphoreType.DMA((2, 3, STAGES)),
            pltpu.SemaphoreType.DMA((2, 3, STAGES)),
        ],
        compiler_params=pltpu.CompilerParams(
            collective_id=0, has_side_effects=True, vmem_limit_bytes=32 * 2**20
        ),
        name="exchange",
    )(
        *(
            pltpu.with_memory_space_constraint(v, pltpu.HBM)
            for v in (
                grad_gate.reshape(ROWS, D), err_gate.reshape(ROWS, D),
                grad_up.reshape(ROWS, D), err_up.reshape(ROWS, D), q_gate.T, q_up.T,
            )
        )
    )
    held = [pltpu.with_memory_space_constraint(v, pltpu.VMEM) for v in made]
    new_err_gate, new_err_up, new_q_gate, new_q_up = pl.pallas_call(
        finish_kernel,
        out_shape=(
            jax.ShapeDtypeStruct((ROWS, D), BF16),
            jax.ShapeDtypeStruct((ROWS, D), BF16),
            jax.ShapeDtypeStruct((RANK, D), F32),
            jax.ShapeDtypeStruct((RANK, D), F32),
        ),
        in_specs=[pl.BlockSpec(memory_space=pltpu.VMEM)] * 6,
        out_specs=[pl.BlockSpec(memory_space=pl.ANY)] * 4,
        scratch_shapes=[
            pltpu.VMEM((ROWS, D), BF16),
            pltpu.VMEM((RANK, D), F32),
            pltpu.VMEM((3 * RANK, 3 * RANK), BF16),
            pltpu.VMEM((ROWS, 4 * RANK), BF16),
            pltpu.SemaphoreType.DMA((4,)),
        ],
        compiler_params=pltpu.CompilerParams(vmem_limit_bytes=12 * 2**20),
        name="finish",
    )(*held)
    return (
        new_err_gate.reshape(1, ROWS, D),
        new_err_up.reshape(1, ROWS, D),
        new_q_gate.T,
        new_q_up.T,
    )


def solution(mesh):
    placed = P("dp", "tensor", None)
    return jax.shard_map(
        body,
        mesh=mesh,
        in_specs=(placed, placed, placed, placed, P(), P()),
        out_specs=(placed, placed, P(), P()),
        check_vma=False,
    )
```

```python
import functools

import jax
import jax.numpy as jnp
from jax import lax
from jax.experimental import pallas as pl
from jax.experimental.pallas import tpu as pltpu
from jax.sharding import PartitionSpec as P

MESH = pl.DeviceIdType.MESH
F32 = jnp.float32
BF16 = jnp.bfloat16
HP = lax.Precision.HIGHEST

DP = 16
TENSOR = 8
D = 7168
ROWS = 256
RANK = 64
HALF = D // 2
CHUNKS = ((0, 2048), (2048, 2048), (4096, 2048), (6144, 1024))
TILE = 256
GROUPS = (
    (0, ((0, 1280, 0), (1280, 1280, 1), (2560, 1024, 2))),
    (1, ((0, 1280, 1), (1280, 1280, 2), (2560, 1024, 0))),
)
NG = len(GROUPS)
BLOCKS = 4
BLOCK = D // BLOCKS
STAGES = 8
CORE_SUM, A_SUM, B_SUM, C_SUM, B_ALL, A_ALL, CORE_ALL, A_FAR = range(STAGES)


SUMS = (CORE_SUM, A_SUM, B_SUM, C_SUM, B_ALL)


def three(value):
    first = value.astype(BF16)
    rest = value - first.astype(F32)
    second = rest.astype(BF16)
    third = (rest - second.astype(F32)).astype(BF16)
    return first, second, third


def nt(left, right, precision=None):
    return lax.dot_general(
        left, right, (((1,), (1,)), ((), ())), precision=precision, preferred_element_type=F32
    )


def nn(left, right, precision=None):
    return jnp.dot(left, right, precision=precision, preferred_element_type=F32)


def finish_stacks(low, left, low_stack, ortho_stack):
    column = jnp.concatenate(three(low), axis=0)
    low_stack[...] = jnp.concatenate([column, column, column], axis=1)
    ortho = nn(low, left, HP).T
    first = ortho.astype(BF16).astype(F32)
    second = ortho - first
    ortho_stack[...] = jnp.concatenate([first, first, second, second], axis=1).astype(BF16)


def finish_block(cols, data, total, low_stack, ortho_stack, err_out, q_out):
    summed = jnp.concatenate(three(total[:, cols]), axis=0)
    terms = nn(low_stack[...], summed)
    new_q = (terms[:RANK] + terms[RANK : 2 * RANK] + terms[2 * RANK :]) * (1.0 / DP)
    q_out[:, cols] = new_q
    first = new_q.astype(BF16)
    second = (new_q - first.astype(F32)).astype(BF16)
    approx = nn(ortho_stack[...], jnp.concatenate([first, second, first, second], axis=0))
    grad = data[:ROWS, cols].astype(F32)
    err = data[ROWS:, cols].astype(F32)
    err_out[:, cols] = (grad + err - approx).astype(BF16)


def exchange_kernel(
    grad_gate, err_gate, grad_up, err_up, q_gate, q_up,
    err_gate_out, q_gate_out, data_up, total_up, left, inverse,
    data_gate, total_gate, low_stack, ortho_stack,
    q_buf, p_acc, p_recv, p_stack, w_send, w_own, w_recv,
    g_part, g_recv, g_all, work, low,
    load_sem, p_send_sem, p_recv_sem, g_send_sem, g_recv_sem, w_send_sem, w_recv_sem,
    *part_refs,
):
    data = (data_gate, data_up)
    total = (total_gate, total_up)
    a_recv, a_sum, b_recv, c_recv = (
        [part_refs[(kind * NG + n) * 3 : (kind * NG + n) * 3 + 3] for n in range(NG)]
        for kind in range(4)
    )
    dp = lax.axis_index("dp")
    t = lax.axis_index("tensor")
    z, x = dp // 4, lax.rem(dp, 4)
    y, core = t // 2, lax.rem(t, 2)
    at = (x, y, z)
    one = dp // DP + 1

    def block(fn, *args):
        lax.fori_loop(0, one, lambda i, carry: (fn(*args), carry)[1], 0)

    def peer(axis, v):
        px, py, pz = (v if axis == i else at[i] for i in range(3))
        return (pz * 4 + px, py * 2 + core)

    def send(src, dst, send_sem, recv_sem, device):
        pltpu.make_async_remote_copy(
            src_ref=src, dst_ref=dst, send_sem=send_sem, recv_sem=recv_sem,
            device_id=device, device_id_type=MESH,
        ).start()

    def arrived(ref, sem):
        pltpu.make_async_copy(ref, ref, sem).wait()

    sources = ((q_gate, grad_gate, err_gate), (q_up, grad_up, err_up))

    def load(g, c, k):
        cols = pl.ds(*CHUNKS[c])
        if k == 0:
            dst = q_buf.at[g, :, cols]
        else:
            dst = data[g].at[pl.ds((k - 1) * ROWS, ROWS), cols]
        return pltpu.make_async_copy(sources[g][k].at[:, cols], dst, load_sem.at[g, c, k])

    for g in range(2):
        for c in range(len(CHUNKS)):
            for k in range(3):
                load(g, c, k).start()

    barrier = pltpu.get_barrier_semaphore()
    for d in range(1, DP):
        pl.semaphore_signal(
            barrier, inc=1, device_id=(lax.rem(dp + d, DP), t), device_id_type=MESH
        )
    for d in range(1, TENSOR):
        pl.semaphore_signal(
            barrier, inc=1, device_id=(dp, lax.rem(t + d, TENSOR)), device_id_type=MESH
        )

    def p_compute(g):
        p_acc[...] = jnp.zeros_like(p_acc)

        def step(c):
            for k in range(3):
                load(g, c, k).wait()
            cols = pl.ds(*CHUNKS[c])
            q3 = jnp.concatenate(three(q_buf[g, :, cols]), axis=0)
            p_acc[...] += nt(data[g][:, cols], q3)

        for c in range(len(CHUNKS)):
            block(step, c)
        both = p_acc[:ROWS, :] + p_acc[ROWS:, :]
        turned = both.T
        summed = turned[:RANK] + turned[RANK : 2 * RANK] + turned[2 * RANK :]
        p_recv[g, 0, 0, x] = summed[: RANK // 2]
        p_recv[g, 0, 1, z] = summed[RANK // 2 :]

    def p_axis(step, h):
        return 0 if step == h else 2

    def p_start(g, step):
        for h in range(2):
            axis = p_axis(step, h)
            mine = p_recv.at[g, step, h, at[axis]]
            for d in (2, 1, 3):
                send(
                    mine, mine, p_send_sem.at[g, step, h], p_recv_sem.at[g, step, h],
                    peer(axis, lax.rem(at[axis] + d, 4)),
                )

    def p_sum(g, step, h):
        arrived(p_recv.at[g, step, h, pl.ds(0, 3)], p_recv_sem.at[g, step, h])
        return (
            p_recv[g, step, h, 0] + p_recv[g, step, h, 1]
            + p_recv[g, step, h, 2] + p_recv[g, step, h, 3]
        )

    def p_turn(g):
        for h in range(2):
            p_recv[g, 1, h, at[p_axis(1, h)]] = p_sum(g, 0, h)
        p_start(g, 1)

    def p_done(g):
        for h in range(2):
            left[g, h * (RANK // 2) : (h + 1) * (RANK // 2)] = p_sum(g, 1, h)
        p3 = jnp.concatenate(three(left[g]), axis=0)
        p_stack[g, :, :ROWS] = p3
        p_stack[g, :, ROWS:] = p3

    def w_block(n, dst, half, p):
        g, parts = GROUPS[n]
        first, width, _ = parts[p]
        start = pl.multiple_of(half * HALF + first, 128)
        for i in range(width // TILE):
            cols = pl.ds(pl.multiple_of(start + i * TILE, 128), TILE)
            prod = nn(p_stack[g], data[g][:, cols])
            dst[g, :, first + i * TILE : first + (i + 1) * TILE] = (
                prod[:RANK] + prod[RANK : 2 * RANK] + prod[2 * RANK :]
            )

    def sems(n, p, stage):
        return w_send_sem.at[n, p, stage], w_recv_sem.at[n, p, stage]

    def axes_of(n, p):
        first = GROUPS[n][1][p][2]
        return first, (first + 1) % 3, (first + 2) % 3

    def half_part(ref, n, p):
        g, parts = GROUPS[n]
        first, width, _ = parts[p]
        return ref.at[g, :, first : first + width]

    def total_part(n, p, rows, skip, width):
        g, parts = GROUPS[n]
        col = pl.multiple_of(core * HALF + parts[p][0] + skip, 128)
        return total[g].at[rows, pl.ds(col, width)]

    def total_block(n, p, v):
        rows = pl.ds(pl.multiple_of(16 * v, 16), 16)
        return total_part(n, p, rows, 0, GROUPS[n][1][p][1])

    def total_leaf(n, p):
        a, b, _ = axes_of(n, p)
        half = GROUPS[n][1][p][1] // 2
        rows = pl.ds(pl.multiple_of(16 * at[a] + 8 * (at[b] // 2), 8), 8)
        return total_part(n, p, rows, half * lax.rem(at[b], 2), half)

    def leaf_rows(v):
        return pl.ds(pl.multiple_of(8 * (v // 2), 8), 8)

    def leaf_cols(n, p, v):
        half = GROUPS[n][1][p][1] // 2
        return pl.ds(pl.multiple_of(half * lax.rem(v, 2), 128), half)

    other_core = (dp, y * 2 + 1 - core)

    def core_start(n):
        def other(p):
            w_block(n, w_send, 1 - core, p)
            send(
                half_part(w_send, n, p), half_part(w_recv, n, p), *sems(n, p, CORE_SUM), other_core
            )

        def rest():
            for p in range(3):
                w_block(n, w_own, core, p)

        for p in range(3):
            block(other, p)
        block(rest)

    def a_start(n):
        def step(p):
            a, _, _ = axes_of(n, p)
            mine, theirs = half_part(w_own, n, p), half_part(w_recv, n, p)
            arrived(theirs, w_recv_sem.at[n, p, CORE_SUM])
            mine[...] += theirs[...]
            for d in (2, 1, 3):
                v = lax.rem(at[a] + d, 4)
                send(
                    mine.at[pl.ds(pl.multiple_of(16 * v, 16), 16)], a_recv[n][p].at[d - 1],
                    *sems(n, p, A_SUM), peer(a, v),
                )

        for p in range(3):
            block(step, p)

    def b_start(n):
        def step(p):
            a, b, _ = axes_of(n, p)
            arrived(a_recv[n][p], w_recv_sem.at[n, p, A_SUM])
            mine = half_part(w_own, n, p).at[pl.ds(pl.multiple_of(16 * at[a], 16), 16)]
            a_sum[n][p][...] = mine[...] + a_recv[n][p][0] + a_recv[n][p][1] + a_recv[n][p][2]
            for d in (2, 1, 3):
                v = lax.rem(at[b] + d, 4)
                send(
                    a_sum[n][p].at[leaf_rows(v), leaf_cols(n, p, v)], b_recv[n][p].at[d - 1],
                    *sems(n, p, B_SUM), peer(b, v),
                )

        for p in range(3):
            block(step, p)

    def c_start(n):
        def step(p):
            _, b, c = axes_of(n, p)
            arrived(b_recv[n][p], w_recv_sem.at[n, p, B_SUM])
            c_recv[n][p][at[c]] = (
                a_sum[n][p][leaf_rows(at[b]), leaf_cols(n, p, at[b])]
                + b_recv[n][p][0] + b_recv[n][p][1] + b_recv[n][p][2]
            )
            mine = c_recv[n][p].at[at[c]]
            for d in (2, 1, 3):
                send(mine, mine, *sems(n, p, C_SUM), peer(c, lax.rem(at[c] + d, 4)))

        for p in range(3):
            block(step, p)

    def b_all_start(n):
        def step(p):
            _, b, _ = axes_of(n, p)
            arrived(c_recv[n][p].at[pl.ds(0, 3)], w_recv_sem.at[n, p, C_SUM])
            leaf = total_leaf(n, p)
            parts = c_recv[n][p]
            leaf[...] = parts[0] + parts[1] + parts[2] + parts[3]
            for d in (2, 1, 3):
                send(leaf, leaf, *sems(n, p, B_ALL), peer(b, lax.rem(at[b] + d, 4)))

        for p in range(3):
            block(step, p)

    def a_all_start(n):
        def step(p):
            a, _, _ = axes_of(n, p)
            arrived(b_recv[n][p], w_recv_sem.at[n, p, B_ALL])
            mine = total_block(n, p, at[a])
            for d in (2, 1, 3):
                send(
                    mine, mine, w_send_sem.at[n, p, A_ALL],
                    w_recv_sem.at[n, p, A_FAR if d == 2 else A_ALL],
                    peer(a, lax.rem(at[a] + d, 4)),
                )
            send(mine, mine, *sems(n, p, CORE_ALL), other_core)

        for p in range(3):
            block(step, p)

    def core_all_start(n):
        def far(p):
            a, _, _ = axes_of(n, p)
            arrived(a_recv[n][p].at[0], w_recv_sem.at[n, p, A_FAR])
            there = total_block(n, p, lax.rem(at[a] + 2, 4))
            send(there, there, *sems(n, p, CORE_ALL), other_core)

        def near(p):
            a, _, _ = axes_of(n, p)
            arrived(a_recv[n][p].at[pl.ds(0, 2)], w_recv_sem.at[n, p, A_ALL])
            for d in (1, 3):
                there = total_block(n, p, lax.rem(at[a] + d, 4))
                send(there, there, *sems(n, p, CORE_ALL), other_core)

        for p in range(3):
            block(far, p)
        for p in range(3):
            block(near, p)

    def core_all_done(n):
        for p in range(3):
            arrived(half_part(w_recv, n, p), w_recv_sem.at[n, p, CORE_ALL])

    member = lax.rem(dp, 8)
    mine = pl.ds(pl.multiple_of(8 * member, 8), 8)

    def gram_start():
        for g in range(2):
            g_part[:, g * RANK : (g + 1) * RANK] = nt(left[g], left[g], HP)
        for d in range(1, TENSOR):
            send(
                g_part.at[mine, :], g_recv.at[t],
                g_send_sem.at[0], g_recv_sem.at[0], (dp, lax.rem(t + d, TENSOR)),
            )
        g_recv[t] = g_part[mine, :]

    def gram_all_start():
        arrived(g_recv.at[pl.ds(0, 7)], g_recv_sem.at[0])
        summed = g_recv[0]
        for i in range(1, TENSOR):
            summed = summed + g_recv[i]
        g_all[mine, :] = summed
        for d in range(1, 8):
            other = 8 * (dp // 8) + lax.rem(member + d, 8)
            send(
                g_all.at[mine, :], g_all.at[mine, :],
                g_send_sem.at[1], g_recv_sem.at[1], (other, t),
            )

    lane = lax.broadcasted_iota(jnp.int32, (RANK, 2 * RANK), 1)
    row = lax.broadcasted_iota(jnp.int32, (RANK, 2 * RANK), 0)
    lane_one = lax.broadcasted_iota(jnp.int32, (1, 2 * RANK), 1)

    def gram_done():
        arrived(g_recv.at[pl.ds(0, 7)], g_recv_sem.at[1])
        work[...] = g_all[...]
        low[...] = jnp.where(lax.rem(lane, RANK) == row, 1.0, 0.0).astype(F32)

    def halves(value, lanes, column):
        gate = jnp.sum(jnp.where(lanes == column, value, 0.0), axis=1, keepdims=True)
        up = jnp.sum(jnp.where(lanes == column + RANK, value, 0.0), axis=1, keepdims=True)
        return jnp.where(lanes < RANK, gate, up)

    def eliminate(first, last):
        def step(j, carry):
            value = work[...]
            pivot_row = work[pl.ds(j, 1), :]
            low_row = low[pl.ds(j, 1), :]
            scale = 1.0 / halves(pivot_row, lane_one, j)
            factor = jnp.where(row > j, halves(value, lane, j) * scale, 0.0)
            work[...] = value - factor * pivot_row
            low[...] = low[...] - factor * low_row
            return carry

        lax.fori_loop(first, last, step, 0)

    def inverse_done():
        value = work[...]
        on = lax.rem(lane, RANK) == row
        gate = jnp.sum(jnp.where(on & (lane < RANK), value, 0.0), axis=1, keepdims=True)
        up = jnp.sum(jnp.where(on & (lane >= RANK), value, 0.0), axis=1, keepdims=True)
        diagonal = jnp.where(lane < RANK, gate, up)
        inverse[...] = low[...] / jnp.sqrt(diagonal)

    def finish_gate():
        finish_stacks(inverse[:, :RANK], left[0], low_stack, ortho_stack)
        for i in range(BLOCKS):
            finish_block(
                slice(i * BLOCK, (i + 1) * BLOCK), data_gate, total_gate, low_stack, ortho_stack,
                err_gate_out, q_gate_out,
            )

    def p_sent():
        for g in range(2):
            for step in range(2):
                for h in range(2):
                    arrived(p_recv.at[g, step, h, pl.ds(0, 3)], p_send_sem.at[g, step, h])
        for phase in range(2):
            arrived(g_recv.at[pl.ds(0, 7)], g_send_sem.at[phase])

    def w_sent(n, stages):
        for p in range(3):
            half = half_part(w_recv, n, p)
            refs = {CORE_SUM: half, CORE_ALL: half, A_SUM: a_recv[n][p], A_ALL: a_recv[n][p]}
            for stage in stages:
                arrived(refs.get(stage, b_recv[n][p]), w_send_sem.at[n, p, stage])

    p_compute(0)
    pl.semaphore_wait(barrier, DP + TENSOR - 2)
    p_start(0, 0)
    p_compute(1)
    p_start(1, 0)
    block(p_turn, 0)
    block(p_turn, 1)
    block(p_done, 0)
    core_start(0)
    a_start(0)
    block(p_done, 1)
    core_start(1)
    block(gram_start)
    a_start(1)
    b_start(0)
    block(gram_all_start)
    b_start(1)
    c_start(0)
    block(gram_done)
    eliminate(0, 16)
    c_start(1)
    b_all_start(0)
    eliminate(16, 32)
    b_all_start(1)
    a_all_start(0)
    eliminate(32, 42)
    a_all_start(1)
    eliminate(42, RANK)
    block(inverse_done)
    core_all_start(0)
    block(p_sent)
    for n in range(NG):
        block(w_sent, n, SUMS)
    core_all_start(1)
    core_all_done(0)
    block(finish_gate)
    core_all_done(1)
    for n in range(NG):
        block(w_sent, n, (A_ALL, CORE_ALL))


def finish_kernel(
    err_gate, q_gate, data, total, left, inverse,
    new_err_gate, new_err_up, new_q_gate, new_q_up,
    err_up, q_up, low_stack, ortho_stack, sem,
):
    gate = (
        pltpu.make_async_copy(err_gate, new_err_gate, sem.at[0]),
        pltpu.make_async_copy(q_gate, new_q_gate, sem.at[1]),
    )
    for copy in gate:
        copy.start()
    finish_stacks(inverse[:, RANK:], left[1], low_stack, ortho_stack)

    def copies(i):
        cols = pl.ds(pl.multiple_of(i * BLOCK, BLOCK), BLOCK)
        return (
            pltpu.make_async_copy(err_up.at[:, cols], new_err_up.at[:, cols], sem.at[2]),
            pltpu.make_async_copy(q_up.at[:, cols], new_q_up.at[:, cols], sem.at[3]),
        )

    def step(i, carry):
        finish_block(
            pl.ds(pl.multiple_of(i * BLOCK, BLOCK), BLOCK), data, total, low_stack, ortho_stack,
            err_up, q_up,
        )
        for copy in copies(i):
            copy.start()
        return carry

    lax.fori_loop(0, BLOCKS, step, 0)
    for copy in gate:
        copy.wait()
    pltpu.make_async_copy(err_up, new_err_up, sem.at[2]).wait()
    pltpu.make_async_copy(q_up, new_q_up, sem.at[3]).wait()


def body(grad_gate, grad_up, err_gate, err_up, q_gate, q_up):
    def part_scratch(lead, rows, divide):
        return [
            pltpu.VMEM(lead + (rows, width // divide), F32)
            for _, parts in GROUPS
            for _, width, _ in parts
        ]

    made = pl.pallas_call(
        exchange_kernel,
        out_shape=(
            pltpu.VMEM((ROWS, D), BF16),
            pltpu.VMEM((RANK, D), F32),
            pltpu.VMEM((2 * ROWS, D), BF16),
            pltpu.VMEM((RANK, D), F32),
            pltpu.VMEM((2, RANK, ROWS), F32),
            pltpu.VMEM((RANK, 2 * RANK), F32),
        ),
        in_specs=[pl.BlockSpec(memory_space=pl.ANY)] * 6,
        out_specs=[pl.BlockSpec(memory_space=pltpu.VMEM)] * 6,
        scratch_shapes=[
            pltpu.VMEM((2 * ROWS, D), BF16),
            pltpu.VMEM((RANK, D), F32),
            pltpu.VMEM((3 * RANK, 3 * RANK), BF16),
            pltpu.VMEM((ROWS, 4 * RANK), BF16),
            pltpu.VMEM((2, RANK, D), F32),
            pltpu.VMEM((2 * ROWS, 3 * RANK), F32),
            pltpu.VMEM((2, 2, 2, 4, RANK // 2, ROWS), F32),
            pltpu.VMEM((2, 3 * RANK, 2 * ROWS), BF16),
            pltpu.VMEM((2, RANK, HALF), F32),
            pltpu.VMEM((2, RANK, HALF), F32),
            pltpu.VMEM((2, RANK, HALF), F32),
            pltpu.VMEM((RANK, 2 * RANK), F32),
            pltpu.VMEM((TENSOR, 8, 2 * RANK), F32),
            pltpu.VMEM((RANK, 2 * RANK), F32),
            pltpu.VMEM((RANK, 2 * RANK), F32),
            pltpu.VMEM((RANK, 2 * RANK), F32),
            pltpu.SemaphoreType.DMA((2, len(CHUNKS), 3)),
            pltpu.SemaphoreType.DMA((2, 2, 2)),
            pltpu.SemaphoreType.DMA((2, 2, 2)),
            pltpu.SemaphoreType.DMA((2,)),
            pltpu.SemaphoreType.DMA((2,)),
            pltpu.SemaphoreType.DMA((NG, 3, STAGES)),
            pltpu.SemaphoreType.DMA((NG, 3, STAGES)),
            *part_scratch((3,), 16, 1),
            *part_scratch((), 16, 1),
            *part_scratch((3,), 8, 2),
            *part_scratch((4,), 8, 2),
        ],
        compiler_params=pltpu.CompilerParams(
            collective_id=0, has_side_effects=True, vmem_limit_bytes=32 * 2**20
        ),
        name="exchange",
    )(
        *(
            pltpu.with_memory_space_constraint(v, pltpu.HBM)
            for v in (
                grad_gate.reshape(ROWS, D), err_gate.reshape(ROWS, D),
                grad_up.reshape(ROWS, D), err_up.reshape(ROWS, D), q_gate.T, q_up.T,
            )
        )
    )
    held = [pltpu.with_memory_space_constraint(v, pltpu.VMEM) for v in made]
    new_err_gate, new_err_up, new_q_gate, new_q_up = pl.pallas_call(
        finish_kernel,
        out_shape=(
            jax.ShapeDtypeStruct((ROWS, D), BF16),
            jax.ShapeDtypeStruct((ROWS, D), BF16),
            jax.ShapeDtypeStruct((RANK, D), F32),
            jax.ShapeDtypeStruct((RANK, D), F32),
        ),
        in_specs=[pl.BlockSpec(memory_space=pltpu.VMEM)] * 6,
        out_specs=[pl.BlockSpec(memory_space=pl.ANY)] * 4,
        scratch_shapes=[
            pltpu.VMEM((ROWS, D), BF16),
            pltpu.VMEM((RANK, D), F32),
            pltpu.VMEM((3 * RANK, 3 * RANK), BF16),
            pltpu.VMEM((ROWS, 4 * RANK), BF16),
            pltpu.SemaphoreType.DMA((4,)),
        ],
        compiler_params=pltpu.CompilerParams(vmem_limit_bytes=12 * 2**20),
        name="finish",
    )(*held)
    return (
        new_err_gate.reshape(1, ROWS, D),
        new_err_up.reshape(1, ROWS, D),
        new_q_gate.T,
        new_q_up.T,
    )


def solution(mesh):
    placed = P("dp", "tensor", None)
    return jax.shard_map(
        body,
        mesh=mesh,
        in_specs=(placed, placed, placed, placed, P(), P()),
        out_specs=(placed, placed, P(), P()),
        check_vma=False,
    )
```

```python
import functools

import jax
import jax.numpy as jnp
from jax import lax
from jax.experimental import pallas as pl
from jax.experimental.pallas import tpu as pltpu
from jax.sharding import PartitionSpec as P

MESH = pl.DeviceIdType.MESH
F32 = jnp.float32
BF16 = jnp.bfloat16
HP = lax.Precision.HIGHEST

DP = 16
TENSOR = 8
D = 7168
ROWS = 256
RANK = 64
HALF = D // 2
CHUNKS = ((0, 2048), (2048, 2048), (4096, 2048), (6144, 1024))
TILE = 256
GROUPS = (
    (0, ((0, 1280, 0), (1280, 1280, 1), (2560, 1024, 2))),
    (1, ((0, 1280, 1), (1280, 1280, 2), (2560, 1024, 0))),
)
NG = len(GROUPS)
BLOCKS = 4
BLOCK = D // BLOCKS
STAGES = 8
CORE_SUM, A_SUM, B_SUM, C_SUM, B_ALL, A_ALL, CORE_ALL, A_FAR = range(STAGES)


SUMS = (CORE_SUM, A_SUM, B_SUM, C_SUM, B_ALL)


def three(value):
    first = value.astype(BF16)
    rest = value - first.astype(F32)
    second = rest.astype(BF16)
    third = (rest - second.astype(F32)).astype(BF16)
    return first, second, third


def nt(left, right, precision=None):
    return lax.dot_general(
        left, right, (((1,), (1,)), ((), ())), precision=precision, preferred_element_type=F32
    )


def nn(left, right, precision=None):
    return jnp.dot(left, right, precision=precision, preferred_element_type=F32)


def finish_stacks(low, left, low_stack, ortho_stack):
    column = jnp.concatenate(three(low), axis=0)
    low_stack[...] = jnp.concatenate([column, column, column], axis=1)
    ortho = nn(low, left, HP).T
    first = ortho.astype(BF16).astype(F32)
    second = ortho - first
    ortho_stack[...] = jnp.concatenate([first, first, second, second], axis=1).astype(BF16)


def finish_block(cols, data, total, low_stack, ortho_stack, err_out, q_out):
    summed = jnp.concatenate(three(total[:, cols]), axis=0)
    terms = nn(low_stack[...], summed)
    new_q = (terms[:RANK] + terms[RANK : 2 * RANK] + terms[2 * RANK :]) * (1.0 / DP)
    q_out[:, cols] = new_q
    first = new_q.astype(BF16)
    second = (new_q - first.astype(F32)).astype(BF16)
    approx = nn(ortho_stack[...], jnp.concatenate([first, second, first, second], axis=0))
    grad = data[:ROWS, cols].astype(F32)
    err = data[ROWS:, cols].astype(F32)
    err_out[:, cols] = (grad + err - approx).astype(BF16)


def exchange_kernel(
    grad_gate, err_gate, grad_up, err_up, q_gate, q_up,
    err_gate_out, q_gate_out, data_up, total_up, left, inverse,
    data_gate, total_gate, low_stack, ortho_stack,
    q_buf, p_acc, p_recv, p_stack, w_send, w_own, w_recv,
    g_part, g_recv, g_all, work, low,
    load_sem, p_send_sem, p_recv_sem, g_send_sem, g_recv_sem, w_send_sem, w_recv_sem,
    *part_refs,
):
    data = (data_gate, data_up)
    total = (total_gate, total_up)
    a_recv, a_sum, b_recv, c_recv = (
        [part_refs[(kind * NG + n) * 3 : (kind * NG + n) * 3 + 3] for n in range(NG)]
        for kind in range(4)
    )
    dp = lax.axis_index("dp")
    t = lax.axis_index("tensor")
    z, x = dp // 4, lax.rem(dp, 4)
    y, core = t // 2, lax.rem(t, 2)
    at = (x, y, z)
    one = dp // DP + 1

    def block(fn, *args):
        lax.fori_loop(0, one, lambda i, carry: (fn(*args), carry)[1], 0)

    def peer(axis, v):
        px, py, pz = (v if axis == i else at[i] for i in range(3))
        return (pz * 4 + px, py * 2 + core)

    def send(src, dst, send_sem, recv_sem, device):
        pltpu.make_async_remote_copy(
            src_ref=src, dst_ref=dst, send_sem=send_sem, recv_sem=recv_sem,
            device_id=device, device_id_type=MESH,
        ).start()

    def arrived(ref, sem):
        pltpu.make_async_copy(ref, ref, sem).wait()

    sources = ((q_gate, grad_gate, err_gate), (q_up, grad_up, err_up))

    def load(g, c, k):
        cols = pl.ds(*CHUNKS[c])
        if k == 0:
            dst = q_buf.at[g, :, cols]
        else:
            dst = data[g].at[pl.ds((k - 1) * ROWS, ROWS), cols]
        return pltpu.make_async_copy(sources[g][k].at[:, cols], dst, load_sem.at[g, c, k])

    for g in range(2):
        for c in range(len(CHUNKS)):
            for k in range(3):
                load(g, c, k).start()

    barrier = pltpu.get_barrier_semaphore()
    for d in range(1, DP):
        pl.semaphore_signal(
            barrier, inc=1, device_id=(lax.rem(dp + d, DP), t), device_id_type=MESH
        )
    for d in range(1, TENSOR):
        pl.semaphore_signal(
            barrier, inc=1, device_id=(dp, lax.rem(t + d, TENSOR)), device_id_type=MESH
        )

    def p_compute(g):
        p_acc[...] = jnp.zeros_like(p_acc)

        def step(c):
            for k in range(3):
                load(g, c, k).wait()
            cols = pl.ds(*CHUNKS[c])
            q3 = jnp.concatenate(three(q_buf[g, :, cols]), axis=0)
            p_acc[...] += nt(data[g][:, cols], q3)

        for c in range(len(CHUNKS)):
            block(step, c)
        both = p_acc[:ROWS, :] + p_acc[ROWS:, :]
        turned = both.T
        summed = turned[:RANK] + turned[RANK : 2 * RANK] + turned[2 * RANK :]
        p_recv[g, 0, 0, x] = summed[: RANK // 2]
        p_recv[g, 0, 1, z] = summed[RANK // 2 :]

    def p_axis(step, h):
        return 0 if step == h else 2

    def p_start(g, step):
        for h in range(2):
            axis = p_axis(step, h)
            mine = p_recv.at[g, step, h, at[axis]]
            for d in (2, 1, 3):
                send(
                    mine, mine, p_send_sem.at[g, step, h], p_recv_sem.at[g, step, h],
                    peer(axis, lax.rem(at[axis] + d, 4)),
                )

    def p_sum(g, step, h):
        arrived(p_recv.at[g, step, h, pl.ds(0, 3)], p_recv_sem.at[g, step, h])
        return (
            p_recv[g, step, h, 0] + p_recv[g, step, h, 1]
            + p_recv[g, step, h, 2] + p_recv[g, step, h, 3]
        )

    def p_turn(g):
        for h in range(2):
            p_recv[g, 1, h, at[p_axis(1, h)]] = p_sum(g, 0, h)
        p_start(g, 1)

    def p_done(g):
        for h in range(2):
            left[g, h * (RANK // 2) : (h + 1) * (RANK // 2)] = p_sum(g, 1, h)
        p3 = jnp.concatenate(three(left[g]), axis=0)
        p_stack[g, :, :ROWS] = p3
        p_stack[g, :, ROWS:] = p3

    def w_block(n, dst, half, p):
        g, parts = GROUPS[n]
        first, width, _ = parts[p]
        start = pl.multiple_of(half * HALF + first, 128)
        for i in range(width // TILE):
            cols = pl.ds(pl.multiple_of(start + i * TILE, 128), TILE)
            prod = nn(p_stack[g], data[g][:, cols])
            dst[g, :, first + i * TILE : first + (i + 1) * TILE] = (
                prod[:RANK] + prod[RANK : 2 * RANK] + prod[2 * RANK :]
            )

    def sems(n, p, stage):
        return w_send_sem.at[n, p, stage], w_recv_sem.at[n, p, stage]

    def axes_of(n, p):
        first = GROUPS[n][1][p][2]
        return first, (first + 1) % 3, (first + 2) % 3

    def half_part(ref, n, p):
        g, parts = GROUPS[n]
        first, width, _ = parts[p]
        return ref.at[g, :, first : first + width]

    def total_part(n, p, rows, skip, width):
        g, parts = GROUPS[n]
        col = pl.multiple_of(core * HALF + parts[p][0] + skip, 128)
        return total[g].at[rows, pl.ds(col, width)]

    def total_block(n, p, v):
        rows = pl.ds(pl.multiple_of(16 * v, 16), 16)
        return total_part(n, p, rows, 0, GROUPS[n][1][p][1])

    def total_leaf(n, p):
        a, b, _ = axes_of(n, p)
        half = GROUPS[n][1][p][1] // 2
        rows = pl.ds(pl.multiple_of(16 * at[a] + 8 * (at[b] // 2), 8), 8)
        return total_part(n, p, rows, half * lax.rem(at[b], 2), half)

    def leaf_rows(v):
        return pl.ds(pl.multiple_of(8 * (v // 2), 8), 8)

    def leaf_cols(n, p, v):
        half = GROUPS[n][1][p][1] // 2
        return pl.ds(pl.multiple_of(half * lax.rem(v, 2), 128), half)

    other_core = (dp, y * 2 + 1 - core)

    def core_start(n):
        def other(p):
            w_block(n, w_send, 1 - core, p)
            send(
                half_part(w_send, n, p), half_part(w_recv, n, p), *sems(n, p, CORE_SUM), other_core
            )

        for p in range(3):
            block(other, p)
        block(w_block, n, w_own, core, 0)

    def a_start(n):
        def step(p):
            a, _, _ = axes_of(n, p)
            mine, theirs = half_part(w_own, n, p), half_part(w_recv, n, p)
            arrived(theirs, w_recv_sem.at[n, p, CORE_SUM])
            mine[...] += theirs[...]
            for d in (2, 1, 3):
                v = lax.rem(at[a] + d, 4)
                send(
                    mine.at[pl.ds(pl.multiple_of(16 * v, 16), 16)], a_recv[n][p].at[d - 1],
                    *sems(n, p, A_SUM), peer(a, v),
                )

        block(step, 0)
        for p in (1, 2):
            block(w_block, n, w_own, core, p)
            block(step, p)

    def b_start(n):
        def step(p):
            a, b, _ = axes_of(n, p)
            arrived(a_recv[n][p], w_recv_sem.at[n, p, A_SUM])
            mine = half_part(w_own, n, p).at[pl.ds(pl.multiple_of(16 * at[a], 16), 16)]
            a_sum[n][p][...] = mine[...] + a_recv[n][p][0] + a_recv[n][p][1] + a_recv[n][p][2]
            for d in (2, 1, 3):
                v = lax.rem(at[b] + d, 4)
                send(
                    a_sum[n][p].at[leaf_rows(v), leaf_cols(n, p, v)], b_recv[n][p].at[d - 1],
                    *sems(n, p, B_SUM), peer(b, v),
                )

        for p in range(3):
            block(step, p)

    def c_start(n):
        def step(p):
            _, b, c = axes_of(n, p)
            arrived(b_recv[n][p], w_recv_sem.at[n, p, B_SUM])
            c_recv[n][p][at[c]] = (
                a_sum[n][p][leaf_rows(at[b]), leaf_cols(n, p, at[b])]
                + b_recv[n][p][0] + b_recv[n][p][1] + b_recv[n][p][2]
            )
            mine = c_recv[n][p].at[at[c]]
            for d in (2, 1, 3):
                send(mine, mine, *sems(n, p, C_SUM), peer(c, lax.rem(at[c] + d, 4)))

        for p in range(3):
            block(step, p)

    def b_all_start(n):
        def step(p):
            _, b, _ = axes_of(n, p)
            arrived(c_recv[n][p].at[pl.ds(0, 3)], w_recv_sem.at[n, p, C_SUM])
            leaf = total_leaf(n, p)
            parts = c_recv[n][p]
            leaf[...] = parts[0] + parts[1] + parts[2] + parts[3]
            for d in (2, 1, 3):
                send(leaf, leaf, *sems(n, p, B_ALL), peer(b, lax.rem(at[b] + d, 4)))

        for p in range(3):
            block(step, p)

    def a_all_start(n):
        def step(p):
            a, _, _ = axes_of(n, p)
            arrived(b_recv[n][p], w_recv_sem.at[n, p, B_ALL])
            mine = total_block(n, p, at[a])
            for d in (2, 1, 3):
                send(
                    mine, mine, w_send_sem.at[n, p, A_ALL],
                    w_recv_sem.at[n, p, A_FAR if d == 2 else A_ALL],
                    peer(a, lax.rem(at[a] + d, 4)),
                )
            send(mine, mine, *sems(n, p, CORE_ALL), other_core)

        for p in range(3):
            block(step, p)

    def core_all_start(n):
        def far(p):
            a, _, _ = axes_of(n, p)
            arrived(a_recv[n][p].at[0], w_recv_sem.at[n, p, A_FAR])
            there = total_block(n, p, lax.rem(at[a] + 2, 4))
            send(there, there, *sems(n, p, CORE_ALL), other_core)

        def near(p):
            a, _, _ = axes_of(n, p)
            arrived(a_recv[n][p].at[pl.ds(0, 2)], w_recv_sem.at[n, p, A_ALL])
            for d in (1, 3):
                there = total_block(n, p, lax.rem(at[a] + d, 4))
                send(there, there, *sems(n, p, CORE_ALL), other_core)

        for p in range(3):
            block(far, p)
        for p in range(3):
            block(near, p)

    def core_all_done(n):
        for p in range(3):
            arrived(half_part(w_recv, n, p), w_recv_sem.at[n, p, CORE_ALL])

    member = lax.rem(dp, 8)
    mine = pl.ds(pl.multiple_of(8 * member, 8), 8)

    def gram_start():
        for g in range(2):
            g_part[:, g * RANK : (g + 1) * RANK] = nt(left[g], left[g], HP)
        for d in range(1, TENSOR):
            send(
                g_part.at[mine, :], g_recv.at[t],
                g_send_sem.at[0], g_recv_sem.at[0], (dp, lax.rem(t + d, TENSOR)),
            )
        g_recv[t] = g_part[mine, :]

    def gram_all_start():
        arrived(g_recv.at[pl.ds(0, 7)], g_recv_sem.at[0])
        summed = g_recv[0]
        for i in range(1, TENSOR):
            summed = summed + g_recv[i]
        g_all[mine, :] = summed
        for d in range(1, 8):
            other = 8 * (dp // 8) + lax.rem(member + d, 8)
            send(
                g_all.at[mine, :], g_all.at[mine, :],
                g_send_sem.at[1], g_recv_sem.at[1], (other, t),
            )

    lane = lax.broadcasted_iota(jnp.int32, (RANK, 2 * RANK), 1)
    row = lax.broadcasted_iota(jnp.int32, (RANK, 2 * RANK), 0)
    lane_one = lax.broadcasted_iota(jnp.int32, (1, 2 * RANK), 1)

    def gram_done():
        arrived(g_recv.at[pl.ds(0, 7)], g_recv_sem.at[1])
        work[...] = g_all[...]
        low[...] = jnp.where(lax.rem(lane, RANK) == row, 1.0, 0.0).astype(F32)

    def halves(value, lanes, column):
        gate = jnp.sum(jnp.where(lanes == column, value, 0.0), axis=1, keepdims=True)
        up = jnp.sum(jnp.where(lanes == column + RANK, value, 0.0), axis=1, keepdims=True)
        return jnp.where(lanes < RANK, gate, up)

    def eliminate(first, last):
        def step(j, carry):
            value = work[...]
            pivot_row = work[pl.ds(j, 1), :]
            low_row = low[pl.ds(j, 1), :]
            scale = 1.0 / halves(pivot_row, lane_one, j)
            factor = jnp.where(row > j, halves(value, lane, j) * scale, 0.0)
            work[...] = value - factor * pivot_row
            low[...] = low[...] - factor * low_row
            return carry

        lax.fori_loop(first, last, step, 0)

    def inverse_done():
        value = work[...]
        on = lax.rem(lane, RANK) == row
        gate = jnp.sum(jnp.where(on & (lane < RANK), value, 0.0), axis=1, keepdims=True)
        up = jnp.sum(jnp.where(on & (lane >= RANK), value, 0.0), axis=1, keepdims=True)
        diagonal = jnp.where(lane < RANK, gate, up)
        inverse[...] = low[...] / jnp.sqrt(diagonal)

    def finish_gate():
        finish_stacks(inverse[:, :RANK], left[0], low_stack, ortho_stack)
        for i in range(BLOCKS):
            finish_block(
                slice(i * BLOCK, (i + 1) * BLOCK), data_gate, total_gate, low_stack, ortho_stack,
                err_gate_out, q_gate_out,
            )

    def p_sent():
        for g in range(2):
            for step in range(2):
                for h in range(2):
                    arrived(p_recv.at[g, step, h, pl.ds(0, 3)], p_send_sem.at[g, step, h])
        for phase in range(2):
            arrived(g_recv.at[pl.ds(0, 7)], g_send_sem.at[phase])

    def w_sent(n, stages):
        for p in range(3):
            half = half_part(w_recv, n, p)
            refs = {CORE_SUM: half, CORE_ALL: half, A_SUM: a_recv[n][p], A_ALL: a_recv[n][p]}
            for stage in stages:
                arrived(refs.get(stage, b_recv[n][p]), w_send_sem.at[n, p, stage])

    p_compute(0)
    pl.semaphore_wait(barrier, DP + TENSOR - 2)
    p_start(0, 0)
    p_compute(1)
    p_start(1, 0)
    block(p_turn, 0)
    block(p_turn, 1)
    block(p_done, 0)
    core_start(0)
    a_start(0)
    block(p_done, 1)
    core_start(1)
    block(gram_start)
    a_start(1)
    b_start(0)
    block(gram_all_start)
    b_start(1)
    c_start(0)
    block(gram_done)
    eliminate(0, 16)
    c_start(1)
    b_all_start(0)
    eliminate(16, 32)
    b_all_start(1)
    a_all_start(0)
    eliminate(32, 42)
    a_all_start(1)
    eliminate(42, RANK)
    block(inverse_done)
    core_all_start(0)
    block(p_sent)
    for n in range(NG):
        block(w_sent, n, SUMS)
    core_all_start(1)
    core_all_done(0)
    block(finish_gate)
    core_all_done(1)
    for n in range(NG):
        block(w_sent, n, (A_ALL, CORE_ALL))


def finish_kernel(
    err_gate, q_gate, data, total, left, inverse,
    new_err_gate, new_err_up, new_q_gate, new_q_up,
    err_up, q_up, low_stack, ortho_stack, sem,
):
    gate = (
        pltpu.make_async_copy(err_gate, new_err_gate, sem.at[0]),
        pltpu.make_async_copy(q_gate, new_q_gate, sem.at[1]),
    )
    for copy in gate:
        copy.start()
    finish_stacks(inverse[:, RANK:], left[1], low_stack, ortho_stack)

    def copies(i):
        cols = pl.ds(pl.multiple_of(i * BLOCK, BLOCK), BLOCK)
        return (
            pltpu.make_async_copy(err_up.at[:, cols], new_err_up.at[:, cols], sem.at[2]),
            pltpu.make_async_copy(q_up.at[:, cols], new_q_up.at[:, cols], sem.at[3]),
        )

    def step(i, carry):
        finish_block(
            pl.ds(pl.multiple_of(i * BLOCK, BLOCK), BLOCK), data, total, low_stack, ortho_stack,
            err_up, q_up,
        )
        for copy in copies(i):
            copy.start()
        return carry

    lax.fori_loop(0, BLOCKS, step, 0)
    for copy in gate:
        copy.wait()
    pltpu.make_async_copy(err_up, new_err_up, sem.at[2]).wait()
    pltpu.make_async_copy(q_up, new_q_up, sem.at[3]).wait()


def body(grad_gate, grad_up, err_gate, err_up, q_gate, q_up):
    def part_scratch(lead, rows, divide):
        return [
            pltpu.VMEM(lead + (rows, width // divide), F32)
            for _, parts in GROUPS
            for _, width, _ in parts
        ]

    made = pl.pallas_call(
        exchange_kernel,
        out_shape=(
            pltpu.VMEM((ROWS, D), BF16),
            pltpu.VMEM((RANK, D), F32),
            pltpu.VMEM((2 * ROWS, D), BF16),
            pltpu.VMEM((RANK, D), F32),
            pltpu.VMEM((2, RANK, ROWS), F32),
            pltpu.VMEM((RANK, 2 * RANK), F32),
        ),
        in_specs=[pl.BlockSpec(memory_space=pl.ANY)] * 6,
        out_specs=[pl.BlockSpec(memory_space=pltpu.VMEM)] * 6,
        scratch_shapes=[
            pltpu.VMEM((2 * ROWS, D), BF16),
            pltpu.VMEM((RANK, D), F32),
            pltpu.VMEM((3 * RANK, 3 * RANK), BF16),
            pltpu.VMEM((ROWS, 4 * RANK), BF16),
            pltpu.VMEM((2, RANK, D), F32),
            pltpu.VMEM((2 * ROWS, 3 * RANK), F32),
            pltpu.VMEM((2, 2, 2, 4, RANK // 2, ROWS), F32),
            pltpu.VMEM((2, 3 * RANK, 2 * ROWS), BF16),
            pltpu.VMEM((2, RANK, HALF), F32),
            pltpu.VMEM((2, RANK, HALF), F32),
            pltpu.VMEM((2, RANK, HALF), F32),
            pltpu.VMEM((RANK, 2 * RANK), F32),
            pltpu.VMEM((TENSOR, 8, 2 * RANK), F32),
            pltpu.VMEM((RANK, 2 * RANK), F32),
            pltpu.VMEM((RANK, 2 * RANK), F32),
            pltpu.VMEM((RANK, 2 * RANK), F32),
            pltpu.SemaphoreType.DMA((2, len(CHUNKS), 3)),
            pltpu.SemaphoreType.DMA((2, 2, 2)),
            pltpu.SemaphoreType.DMA((2, 2, 2)),
            pltpu.SemaphoreType.DMA((2,)),
            pltpu.SemaphoreType.DMA((2,)),
            pltpu.SemaphoreType.DMA((NG, 3, STAGES)),
            pltpu.SemaphoreType.DMA((NG, 3, STAGES)),
            *part_scratch((3,), 16, 1),
            *part_scratch((), 16, 1),
            *part_scratch((3,), 8, 2),
            *part_scratch((4,), 8, 2),
        ],
        compiler_params=pltpu.CompilerParams(
            collective_id=0, has_side_effects=True, vmem_limit_bytes=32 * 2**20
        ),
        name="exchange",
    )(
        *(
            pltpu.with_memory_space_constraint(v, pltpu.HBM)
            for v in (
                grad_gate.reshape(ROWS, D), err_gate.reshape(ROWS, D),
                grad_up.reshape(ROWS, D), err_up.reshape(ROWS, D), q_gate.T, q_up.T,
            )
        )
    )
    held = [pltpu.with_memory_space_constraint(v, pltpu.VMEM) for v in made]
    new_err_gate, new_err_up, new_q_gate, new_q_up = pl.pallas_call(
        finish_kernel,
        out_shape=(
            jax.ShapeDtypeStruct((ROWS, D), BF16),
            jax.ShapeDtypeStruct((ROWS, D), BF16),
            jax.ShapeDtypeStruct((RANK, D), F32),
            jax.ShapeDtypeStruct((RANK, D), F32),
        ),
        in_specs=[pl.BlockSpec(memory_space=pltpu.VMEM)] * 6,
        out_specs=[pl.BlockSpec(memory_space=pl.ANY)] * 4,
        scratch_shapes=[
            pltpu.VMEM((ROWS, D), BF16),
            pltpu.VMEM((RANK, D), F32),
            pltpu.VMEM((3 * RANK, 3 * RANK), BF16),
            pltpu.VMEM((ROWS, 4 * RANK), BF16),
            pltpu.SemaphoreType.DMA((4,)),
        ],
        compiler_params=pltpu.CompilerParams(vmem_limit_bytes=12 * 2**20),
        name="finish",
    )(*held)
    return (
        new_err_gate.reshape(1, ROWS, D),
        new_err_up.reshape(1, ROWS, D),
        new_q_gate.T,
        new_q_up.T,
    )


def solution(mesh):
    placed = P("dp", "tensor", None)
    return jax.shard_map(
        body,
        mesh=mesh,
        in_specs=(placed, placed, placed, placed, P(), P()),
        out_specs=(placed, placed, P(), P()),
        check_vma=False,
    )
```

```python
import functools

import jax
import jax.numpy as jnp
from jax import lax
from jax.experimental import pallas as pl
from jax.experimental.pallas import tpu as pltpu
from jax.sharding import PartitionSpec as P

MESH = pl.DeviceIdType.MESH
F32 = jnp.float32
BF16 = jnp.bfloat16
HP = lax.Precision.HIGHEST

DP = 16
TENSOR = 8
D = 7168
ROWS = 256
RANK = 64
HALF = D // 2
CHUNKS = ((0, 2048), (2048, 2048), (4096, 2048), (6144, 1024))
TILE = 256
GROUPS = (
    (0, ((0, 1280, 0), (1280, 1280, 1), (2560, 1024, 2))),
    (1, ((0, 1280, 1), (1280, 1280, 2), (2560, 1024, 0))),
)
NG = len(GROUPS)
BLOCKS = 4
BLOCK = D // BLOCKS
STAGES = 8
CORE_SUM, A_SUM, B_SUM, C_SUM, B_ALL, A_ALL, CORE_ALL, A_FAR = range(STAGES)


SUMS = (CORE_SUM, A_SUM, B_SUM, C_SUM, B_ALL)


def three(value):
    first = value.astype(BF16)
    rest = value - first.astype(F32)
    second = rest.astype(BF16)
    third = (rest - second.astype(F32)).astype(BF16)
    return first, second, third


def nt(left, right, precision=None):
    return lax.dot_general(
        left, right, (((1,), (1,)), ((), ())), precision=precision, preferred_element_type=F32
    )


def nn(left, right, precision=None):
    return jnp.dot(left, right, precision=precision, preferred_element_type=F32)


def finish_stacks(low, left, low_stack, ortho_stack):
    column = jnp.concatenate(three(low), axis=0)
    low_stack[...] = jnp.concatenate([column, column, column], axis=1)
    ortho = nn(low, left, HP).T
    first = ortho.astype(BF16).astype(F32)
    second = ortho - first
    ortho_stack[...] = jnp.concatenate([first, first, second, second], axis=1).astype(BF16)


def finish_block(cols, data, total, low_stack, ortho_stack, err_out, q_out):
    summed = jnp.concatenate(three(total[:, cols]), axis=0)
    terms = nn(low_stack[...], summed)
    new_q = (terms[:RANK] + terms[RANK : 2 * RANK] + terms[2 * RANK :]) * (1.0 / DP)
    q_out[:, cols] = new_q
    first = new_q.astype(BF16)
    second = (new_q - first.astype(F32)).astype(BF16)
    approx = nn(ortho_stack[...], jnp.concatenate([first, second, first, second], axis=0))
    grad = data[:ROWS, cols].astype(F32)
    err = data[ROWS:, cols].astype(F32)
    err_out[:, cols] = (grad + err - approx).astype(BF16)


def exchange_kernel(
    grad_gate, err_gate, grad_up, err_up, q_gate, q_up,
    err_gate_out, q_gate_out, data_up, total_up, left, inverse,
    data_gate, total_gate, low_stack, ortho_stack,
    q_buf, p_acc, p_recv, p_stack, w_send, w_own, w_recv,
    g_part, g_recv, g_all, work, low,
    load_sem, p_send_sem, p_recv_sem, g_send_sem, g_recv_sem, w_send_sem, w_recv_sem,
    *part_refs,
):
    data = (data_gate, data_up)
    total = (total_gate, total_up)
    a_recv, a_sum, b_recv, c_recv = (
        [part_refs[(kind * NG + n) * 3 : (kind * NG + n) * 3 + 3] for n in range(NG)]
        for kind in range(4)
    )
    dp = lax.axis_index("dp")
    t = lax.axis_index("tensor")
    z, x = dp // 4, lax.rem(dp, 4)
    y, core = t // 2, lax.rem(t, 2)
    at = (x, y, z)
    one = dp // DP + 1

    def block(fn, *args):
        lax.fori_loop(0, one, lambda i, carry: (fn(*args), carry)[1], 0)

    def peer(axis, v):
        px, py, pz = (v if axis == i else at[i] for i in range(3))
        return (pz * 4 + px, py * 2 + core)

    def send(src, dst, send_sem, recv_sem, device):
        pltpu.make_async_remote_copy(
            src_ref=src, dst_ref=dst, send_sem=send_sem, recv_sem=recv_sem,
            device_id=device, device_id_type=MESH,
        ).start()

    def arrived(ref, sem):
        pltpu.make_async_copy(ref, ref, sem).wait()

    sources = ((q_gate, grad_gate, err_gate), (q_up, grad_up, err_up))

    def load(g, c, k):
        cols = pl.ds(*CHUNKS[c])
        if k == 0:
            dst = q_buf.at[g, :, cols]
        else:
            dst = data[g].at[pl.ds((k - 1) * ROWS, ROWS), cols]
        return pltpu.make_async_copy(sources[g][k].at[:, cols], dst, load_sem.at[g, c, k])

    for g in range(2):
        for c in range(len(CHUNKS)):
            for k in range(3):
                load(g, c, k).start()

    barrier = pltpu.get_barrier_semaphore()
    for d in range(1, DP):
        pl.semaphore_signal(
            barrier, inc=1, device_id=(lax.rem(dp + d, DP), t), device_id_type=MESH
        )
    for d in range(1, TENSOR):
        pl.semaphore_signal(
            barrier, inc=1, device_id=(dp, lax.rem(t + d, TENSOR)), device_id_type=MESH
        )

    def p_compute(g):
        p_acc[...] = jnp.zeros_like(p_acc)

        def step(c):
            for k in range(3):
                load(g, c, k).wait()
            cols = pl.ds(*CHUNKS[c])
            q3 = jnp.concatenate(three(q_buf[g, :, cols]), axis=0)
            p_acc[...] += nt(data[g][:, cols], q3)

        for c in range(len(CHUNKS)):
            block(step, c)
        both = p_acc[:ROWS, :] + p_acc[ROWS:, :]
        turned = both.T
        summed = turned[:RANK] + turned[RANK : 2 * RANK] + turned[2 * RANK :]
        p_recv[g, 0, 0, x] = summed[: RANK // 2]
        p_recv[g, 0, 1, z] = summed[RANK // 2 :]

    def p_axis(step, h):
        return 0 if step == h else 2

    def p_start(g, step):
        for h in range(2):
            axis = p_axis(step, h)
            mine = p_recv.at[g, step, h, at[axis]]
            for d in (2, 1, 3):
                send(
                    mine, mine, p_send_sem.at[g, step, h], p_recv_sem.at[g, step, h],
                    peer(axis, lax.rem(at[axis] + d, 4)),
                )

    def p_sum(g, step, h):
        arrived(p_recv.at[g, step, h, pl.ds(0, 3)], p_recv_sem.at[g, step, h])
        return (
            p_recv[g, step, h, 0] + p_recv[g, step, h, 1]
            + p_recv[g, step, h, 2] + p_recv[g, step, h, 3]
        )

    def p_turn(g):
        for h in range(2):
            p_recv[g, 1, h, at[p_axis(1, h)]] = p_sum(g, 0, h)
        p_start(g, 1)

    def p_done(g):
        for h in range(2):
            left[g, h * (RANK // 2) : (h + 1) * (RANK // 2)] = p_sum(g, 1, h)
        p3 = jnp.concatenate(three(left[g]), axis=0)
        p_stack[g, :, :ROWS] = p3
        p_stack[g, :, ROWS:] = p3

    def w_block(n, dst, half, p):
        g, parts = GROUPS[n]
        first, width, _ = parts[p]
        start = pl.multiple_of(half * HALF + first, 128)
        for i in range(width // TILE):
            cols = pl.ds(pl.multiple_of(start + i * TILE, 128), TILE)
            prod = nn(p_stack[g], data[g][:, cols])
            dst[g, :, first + i * TILE : first + (i + 1) * TILE] = (
                prod[:RANK] + prod[RANK : 2 * RANK] + prod[2 * RANK :]
            )

    def sems(n, p, stage):
        return w_send_sem.at[n, p, stage], w_recv_sem.at[n, p, stage]

    def axes_of(n, p):
        first = GROUPS[n][1][p][2]
        return first, (first + 1) % 3, (first + 2) % 3

    def half_part(ref, n, p):
        g, parts = GROUPS[n]
        first, width, _ = parts[p]
        return ref.at[g, :, first : first + width]

    def total_part(n, p, rows, skip, width):
        g, parts = GROUPS[n]
        col = pl.multiple_of(core * HALF + parts[p][0] + skip, 128)
        return total[g].at[rows, pl.ds(col, width)]

    def total_block(n, p, v):
        rows = pl.ds(pl.multiple_of(16 * v, 16), 16)
        return total_part(n, p, rows, 0, GROUPS[n][1][p][1])

    def total_leaf(n, p):
        a, b, _ = axes_of(n, p)
        half = GROUPS[n][1][p][1] // 2
        rows = pl.ds(pl.multiple_of(16 * at[a] + 8 * (at[b] // 2), 8), 8)
        return total_part(n, p, rows, half * lax.rem(at[b], 2), half)

    def leaf_rows(v):
        return pl.ds(pl.multiple_of(8 * (v // 2), 8), 8)

    def leaf_cols(n, p, v):
        half = GROUPS[n][1][p][1] // 2
        return pl.ds(pl.multiple_of(half * lax.rem(v, 2), 128), half)

    other_core = (dp, y * 2 + 1 - core)

    def core_start(n):
        def other(p):
            w_block(n, w_send, 1 - core, p)
            send(
                half_part(w_send, n, p), half_part(w_recv, n, p), *sems(n, p, CORE_SUM), other_core
            )

        for p in range(3):
            block(other, p)
        block(w_block, n, w_own, core, 0)

    def a_start(n):
        def step(p):
            a, _, _ = axes_of(n, p)
            mine, theirs = half_part(w_own, n, p), half_part(w_recv, n, p)
            arrived(theirs, w_recv_sem.at[n, p, CORE_SUM])
            mine[...] += theirs[...]
            for d in (2, 1, 3):
                v = lax.rem(at[a] + d, 4)
                send(
                    mine.at[pl.ds(pl.multiple_of(16 * v, 16), 16)], a_recv[n][p].at[d - 1],
                    *sems(n, p, A_SUM), peer(a, v),
                )

        block(step, 0)
        for p in (1, 2):
            block(w_block, n, w_own, core, p)
            block(step, p)

    def b_start(n):
        def step(p):
            a, b, _ = axes_of(n, p)
            arrived(a_recv[n][p], w_recv_sem.at[n, p, A_SUM])
            mine = half_part(w_own, n, p).at[pl.ds(pl.multiple_of(16 * at[a], 16), 16)]
            a_sum[n][p][...] = mine[...] + a_recv[n][p][0] + a_recv[n][p][1] + a_recv[n][p][2]
            for d in (2, 1, 3):
                v = lax.rem(at[b] + d, 4)
                send(
                    a_sum[n][p].at[leaf_rows(v), leaf_cols(n, p, v)], b_recv[n][p].at[d - 1],
                    *sems(n, p, B_SUM), peer(b, v),
                )

        for p in range(3):
            block(step, p)

    def c_start(n):
        def step(p):
            _, b, c = axes_of(n, p)
            arrived(b_recv[n][p], w_recv_sem.at[n, p, B_SUM])
            c_recv[n][p][at[c]] = (
                a_sum[n][p][leaf_rows(at[b]), leaf_cols(n, p, at[b])]
                + b_recv[n][p][0] + b_recv[n][p][1] + b_recv[n][p][2]
            )
            mine = c_recv[n][p].at[at[c]]
            for d in (2, 1, 3):
                send(mine, mine, *sems(n, p, C_SUM), peer(c, lax.rem(at[c] + d, 4)))

        for p in range(3):
            block(step, p)

    def b_all_start(n):
        def step(p):
            _, b, _ = axes_of(n, p)
            arrived(c_recv[n][p].at[pl.ds(0, 3)], w_recv_sem.at[n, p, C_SUM])
            leaf = total_leaf(n, p)
            parts = c_recv[n][p]
            leaf[...] = parts[0] + parts[1] + parts[2] + parts[3]
            for d in (2, 1, 3):
                send(leaf, leaf, *sems(n, p, B_ALL), peer(b, lax.rem(at[b] + d, 4)))

        for p in range(3):
            block(step, p)

    def a_all_start(n):
        def step(p):
            a, _, _ = axes_of(n, p)
            arrived(b_recv[n][p], w_recv_sem.at[n, p, B_ALL])
            mine = total_block(n, p, at[a])
            for d in (2, 1, 3):
                send(
                    mine, mine, w_send_sem.at[n, p, A_ALL],
                    w_recv_sem.at[n, p, A_FAR if d == 2 else A_ALL],
                    peer(a, lax.rem(at[a] + d, 4)),
                )
            send(mine, mine, *sems(n, p, CORE_ALL), other_core)

        for p in range(3):
            block(step, p)

    def core_all_start(n):
        def far(p):
            a, _, _ = axes_of(n, p)
            arrived(a_recv[n][p].at[0], w_recv_sem.at[n, p, A_FAR])
            there = total_block(n, p, lax.rem(at[a] + 2, 4))
            send(there, there, *sems(n, p, CORE_ALL), other_core)

        def near(p):
            a, _, _ = axes_of(n, p)
            arrived(a_recv[n][p].at[pl.ds(0, 2)], w_recv_sem.at[n, p, A_ALL])
            for d in (1, 3):
                there = total_block(n, p, lax.rem(at[a] + d, 4))
                send(there, there, *sems(n, p, CORE_ALL), other_core)

        for p in range(3):
            block(far, p)
        for p in range(3):
            block(near, p)

    def core_all_done(n):
        for p in range(3):
            arrived(half_part(w_recv, n, p), w_recv_sem.at[n, p, CORE_ALL])

    member = lax.rem(dp, 8)
    mine = pl.ds(pl.multiple_of(8 * member, 8), 8)

    def gram_start():
        for g in range(2):
            g_part[:, g * RANK : (g + 1) * RANK] = nt(left[g], left[g], HP)
        for d in range(1, TENSOR):
            send(
                g_part.at[mine, :], g_recv.at[t],
                g_send_sem.at[0], g_recv_sem.at[0], (dp, lax.rem(t + d, TENSOR)),
            )
        g_recv[t] = g_part[mine, :]

    def gram_all_start():
        arrived(g_recv.at[pl.ds(0, 7)], g_recv_sem.at[0])
        summed = g_recv[0]
        for i in range(1, TENSOR):
            summed = summed + g_recv[i]
        g_all[mine, :] = summed
        for d in range(1, 8):
            other = 8 * (dp // 8) + lax.rem(member + d, 8)
            send(
                g_all.at[mine, :], g_all.at[mine, :],
                g_send_sem.at[1], g_recv_sem.at[1], (other, t),
            )

    lane = lax.broadcasted_iota(jnp.int32, (RANK, 2 * RANK), 1)
    row = lax.broadcasted_iota(jnp.int32, (RANK, 2 * RANK), 0)
    lane_one = lax.broadcasted_iota(jnp.int32, (1, 2 * RANK), 1)

    def gram_done():
        arrived(g_recv.at[pl.ds(0, 7)], g_recv_sem.at[1])
        work[...] = g_all[...]
        low[...] = jnp.where(lax.rem(lane, RANK) == row, 1.0, 0.0).astype(F32)

    def halves(value, lanes, column):
        gate = jnp.sum(jnp.where(lanes == column, value, 0.0), axis=1, keepdims=True)
        up = jnp.sum(jnp.where(lanes == column + RANK, value, 0.0), axis=1, keepdims=True)
        return jnp.where(lanes < RANK, gate, up)

    def eliminate(first, last):
        def step(j, carry):
            value = work[...]
            pivot_row = work[pl.ds(j, 1), :]
            low_row = low[pl.ds(j, 1), :]
            scale = 1.0 / halves(pivot_row, lane_one, j)
            factor = jnp.where(row > j, halves(value, lane, j) * scale, 0.0)
            work[...] = value - factor * pivot_row
            low[...] = low[...] - factor * low_row
            return carry

        lax.fori_loop(first, last, step, 0)

    def inverse_done():
        value = work[...]
        on = lax.rem(lane, RANK) == row
        gate = jnp.sum(jnp.where(on & (lane < RANK), value, 0.0), axis=1, keepdims=True)
        up = jnp.sum(jnp.where(on & (lane >= RANK), value, 0.0), axis=1, keepdims=True)
        diagonal = jnp.where(lane < RANK, gate, up)
        inverse[...] = low[...] / jnp.sqrt(diagonal)

    def gate_stacks():
        finish_stacks(inverse[:, :RANK], left[0], low_stack, ortho_stack)

    def finish_gate():
        for i in range(BLOCKS):
            finish_block(
                slice(i * BLOCK, (i + 1) * BLOCK), data_gate, total_gate, low_stack, ortho_stack,
                err_gate_out, q_gate_out,
            )

    def p_sent():
        for g in range(2):
            for step in range(2):
                for h in range(2):
                    arrived(p_recv.at[g, step, h, pl.ds(0, 3)], p_send_sem.at[g, step, h])
        for phase in range(2):
            arrived(g_recv.at[pl.ds(0, 7)], g_send_sem.at[phase])

    def w_sent(n, stages):
        for p in range(3):
            half = half_part(w_recv, n, p)
            refs = {CORE_SUM: half, CORE_ALL: half, A_SUM: a_recv[n][p], A_ALL: a_recv[n][p]}
            for stage in stages:
                arrived(refs.get(stage, b_recv[n][p]), w_send_sem.at[n, p, stage])

    p_compute(0)
    pl.semaphore_wait(barrier, DP + TENSOR - 2)
    p_start(0, 0)
    p_compute(1)
    p_start(1, 0)
    block(p_turn, 0)
    block(p_turn, 1)
    block(p_done, 0)
    core_start(0)
    a_start(0)
    block(p_done, 1)
    core_start(1)
    block(gram_start)
    a_start(1)
    b_start(0)
    block(gram_all_start)
    b_start(1)
    c_start(0)
    block(gram_done)
    eliminate(0, 16)
    c_start(1)
    b_all_start(0)
    eliminate(16, 32)
    b_all_start(1)
    a_all_start(0)
    eliminate(32, 42)
    a_all_start(1)
    eliminate(42, RANK)
    block(inverse_done)
    core_all_start(0)
    block(gate_stacks)
    block(p_sent)
    for n in range(NG):
        block(w_sent, n, SUMS)
    core_all_start(1)
    core_all_done(0)
    block(finish_gate)
    core_all_done(1)
    for n in range(NG):
        block(w_sent, n, (A_ALL, CORE_ALL))


def finish_kernel(
    err_gate, q_gate, data, total, left, inverse,
    new_err_gate, new_err_up, new_q_gate, new_q_up,
    err_up, q_up, low_stack, ortho_stack, sem,
):
    gate = (
        pltpu.make_async_copy(err_gate, new_err_gate, sem.at[0]),
        pltpu.make_async_copy(q_gate, new_q_gate, sem.at[1]),
    )
    for copy in gate:
        copy.start()
    finish_stacks(inverse[:, RANK:], left[1], low_stack, ortho_stack)

    def copies(i):
        cols = pl.ds(pl.multiple_of(i * BLOCK, BLOCK), BLOCK)
        return (
            pltpu.make_async_copy(err_up.at[:, cols], new_err_up.at[:, cols], sem.at[2]),
            pltpu.make_async_copy(q_up.at[:, cols], new_q_up.at[:, cols], sem.at[3]),
        )

    def step(i, carry):
        finish_block(
            pl.ds(pl.multiple_of(i * BLOCK, BLOCK), BLOCK), data, total, low_stack, ortho_stack,
            err_up, q_up,
        )
        for copy in copies(i):
            copy.start()
        return carry

    lax.fori_loop(0, BLOCKS, step, 0)
    for copy in gate:
        copy.wait()
    pltpu.make_async_copy(err_up, new_err_up, sem.at[2]).wait()
    pltpu.make_async_copy(q_up, new_q_up, sem.at[3]).wait()


def body(grad_gate, grad_up, err_gate, err_up, q_gate, q_up):
    def part_scratch(lead, rows, divide):
        return [
            pltpu.VMEM(lead + (rows, width // divide), F32)
            for _, parts in GROUPS
            for _, width, _ in parts
        ]

    made = pl.pallas_call(
        exchange_kernel,
        out_shape=(
            pltpu.VMEM((ROWS, D), BF16),
            pltpu.VMEM((RANK, D), F32),
            pltpu.VMEM((2 * ROWS, D), BF16),
            pltpu.VMEM((RANK, D), F32),
            pltpu.VMEM((2, RANK, ROWS), F32),
            pltpu.VMEM((RANK, 2 * RANK), F32),
        ),
        in_specs=[pl.BlockSpec(memory_space=pl.ANY)] * 6,
        out_specs=[pl.BlockSpec(memory_space=pltpu.VMEM)] * 6,
        scratch_shapes=[
            pltpu.VMEM((2 * ROWS, D), BF16),
            pltpu.VMEM((RANK, D), F32),
            pltpu.VMEM((3 * RANK, 3 * RANK), BF16),
            pltpu.VMEM((ROWS, 4 * RANK), BF16),
            pltpu.VMEM((2, RANK, D), F32),
            pltpu.VMEM((2 * ROWS, 3 * RANK), F32),
            pltpu.VMEM((2, 2, 2, 4, RANK // 2, ROWS), F32),
            pltpu.VMEM((2, 3 * RANK, 2 * ROWS), BF16),
            pltpu.VMEM((2, RANK, HALF), F32),
            pltpu.VMEM((2, RANK, HALF), F32),
            pltpu.VMEM((2, RANK, HALF), F32),
            pltpu.VMEM((RANK, 2 * RANK), F32),
            pltpu.VMEM((TENSOR, 8, 2 * RANK), F32),
            pltpu.VMEM((RANK, 2 * RANK), F32),
            pltpu.VMEM((RANK, 2 * RANK), F32),
            pltpu.VMEM((RANK, 2 * RANK), F32),
            pltpu.SemaphoreType.DMA((2, len(CHUNKS), 3)),
            pltpu.SemaphoreType.DMA((2, 2, 2)),
            pltpu.SemaphoreType.DMA((2, 2, 2)),
            pltpu.SemaphoreType.DMA((2,)),
            pltpu.SemaphoreType.DMA((2,)),
            pltpu.SemaphoreType.DMA((NG, 3, STAGES)),
            pltpu.SemaphoreType.DMA((NG, 3, STAGES)),
            *part_scratch((3,), 16, 1),
            *part_scratch((), 16, 1),
            *part_scratch((3,), 8, 2),
            *part_scratch((4,), 8, 2),
        ],
        compiler_params=pltpu.CompilerParams(
            collective_id=0, has_side_effects=True, vmem_limit_bytes=32 * 2**20
        ),
        name="exchange",
    )(
        *(
            pltpu.with_memory_space_constraint(v, pltpu.HBM)
            for v in (
                grad_gate.reshape(ROWS, D), err_gate.reshape(ROWS, D),
                grad_up.reshape(ROWS, D), err_up.reshape(ROWS, D), q_gate.T, q_up.T,
            )
        )
    )
    held = [pltpu.with_memory_space_constraint(v, pltpu.VMEM) for v in made]
    new_err_gate, new_err_up, new_q_gate, new_q_up = pl.pallas_call(
        finish_kernel,
        out_shape=(
            jax.ShapeDtypeStruct((ROWS, D), BF16),
            jax.ShapeDtypeStruct((ROWS, D), BF16),
            jax.ShapeDtypeStruct((RANK, D), F32),
            jax.ShapeDtypeStruct((RANK, D), F32),
        ),
        in_specs=[pl.BlockSpec(memory_space=pltpu.VMEM)] * 6,
        out_specs=[pl.BlockSpec(memory_space=pl.ANY)] * 4,
        scratch_shapes=[
            pltpu.VMEM((ROWS, D), BF16),
            pltpu.VMEM((RANK, D), F32),
            pltpu.VMEM((3 * RANK, 3 * RANK), BF16),
            pltpu.VMEM((ROWS, 4 * RANK), BF16),
            pltpu.SemaphoreType.DMA((4,)),
        ],
        compiler_params=pltpu.CompilerParams(vmem_limit_bytes=12 * 2**20),
        name="finish",
    )(*held)
    return (
        new_err_gate.reshape(1, ROWS, D),
        new_err_up.reshape(1, ROWS, D),
        new_q_gate.T,
        new_q_up.T,
    )


def solution(mesh):
    placed = P("dp", "tensor", None)
    return jax.shard_map(
        body,
        mesh=mesh,
        in_specs=(placed, placed, placed, placed, P(), P()),
        out_specs=(placed, placed, P(), P()),
        check_vma=False,
    )
```
